32 devices in a mesh: group: 2 (over x), expert: 16 (over z, y, core).
Axes of the slice: x: 2, y: 2, z: 4, core: 2. Of those that a mesh axis runs over, the one named last changes fastest.
Arguments:
- hidden_slots: bfloat16 [32, 512, 2048], P(('group', 'expert')), parts along dimension 0, may hold values from -6 to 6
- adapter_in: bfloat16 [16, 16, 2048], P('expert'), may hold values from -8 to 8
- adapter_out: bfloat16 [16, 16, 7168], P('expert'), may hold values from -8 to 8
- expert_ids: int32 [4096, 2], P(('group', 'expert')), parts along dimension 0, may hold values from 0 to 15, all different within a row; in each aligned block of 128 rows (0 to 127, 128 to 255, ...) at most 32 rows name the same one
- gate_weights: float32 [4096, 2], P(('group', 'expert')), parts along dimension 0, may hold values from 0.05 to 0.5
- cotangent: bfloat16 [4096, 7168], P(('group', 'expert')), parts along dimension 0, may hold values from -6 to 6
Outputs:
- adapter_delta: bfloat16 [4096, 7168], P(('group', 'expert')), parts along dimension 0
- scaled_in_grad: float32 [32, 16, 2048], P(('group', 'expert')), parts along dimension 0
- scaled_out_grad: float32 [32, 16, 7168], P(('group', 'expert')), parts along dimension 0
The draws below stay inside these ranges and needn't reach their ends.
There are 2 independent parts, one for each index of `group`. The reference program is written for one: setup_inputs(seed, part) draws one part's arguments, and reference() takes and returns one part's arrays. A program takes and returns all parts, laid end to end along the dimension named above; an argument that names none is the same for every part. Nothing has to cross between parts.
Inputs may be any that keep to these rules, and one draw needn't show every extreme that they name: `expert_ids`: each row names 2 different experts. In each aligned block of 128 rows (the rows of one device) no expert is named by more than 32 rows, a bound that some block reaches.
All inputs are finite; a program needn't handle non-finite values.
Results may differ from the reference program's by a relative error of at most 0.0063.
Values may be sent and summed in bfloat16 or wider, within the bound.
No kernel may reach another device: no remote copies, remote signals or barrier semaphores. Data moves between devices by JAX's collectives and lax.ppermute only.
A program may use at most 128 MiB of HBM per device.

```python
import math
import jax
import jax.numpy as jnp
import numpy as np
from jax import lax

D = 7168
FF = 2048
R = 16
TOP = 2
TOK_DEV = 128
EXPERTS = 16
CAP = 32
TOKENS = 2048
N_EXPERT = 16


def draw_adapter_in(key, part):
    key = jax.random.fold_in(key, 11)
    k_base, k_rows, k_cols = jax.random.split(key, 3)
    steps_along = jnp.arange(EXPERTS, dtype=jnp.float32) / (2.0 * max(EXPERTS - 1, 1))
    base = jax.random.normal(k_base, (EXPERTS, R, FF), jnp.float32)
    rising = 3.0 ** steps_along
    base = jnp.clip(base, -4.0, 4.0)
    row_scale = 10.0 ** jax.random.uniform(k_rows, (EXPERTS, R, 1), jnp.float32, -0.5, 0.5)
    col_scale = 10.0 ** jax.random.uniform(k_cols, (EXPERTS, 1, FF), jnp.float32, -0.5, 0.5)
    return (base * row_scale * col_scale * rising[:, None, None] / (2.1 * FF ** 0.5)).astype(jnp.bfloat16)


def draw_adapter_out(key, part):
    key = jax.random.fold_in(key, 12)
    k_base, k_rows, k_cols = jax.random.split(key, 3)
    steps_along = jnp.arange(EXPERTS, dtype=jnp.float32) / (2.0 * max(EXPERTS - 1, 1))
    base = jax.random.normal(k_base, (EXPERTS, R, D), jnp.float32)
    rising = 3.0 ** steps_along
    base = jnp.clip(base, -4.0, 4.0)
    row_scale = 10.0 ** jax.random.uniform(k_rows, (EXPERTS, R, 1), jnp.float32, -0.5, 0.5)
    col_scale = 10.0 ** jax.random.uniform(k_cols, (EXPERTS, 1, D), jnp.float32, -0.5, 0.5)
    return (base * row_scale * col_scale * rising[:, None, None] / (2.1 * D ** 0.5)).astype(jnp.bfloat16)


def level_of(key, dims, pieces, smallest, high):
    def one(dim, shards_of):
        heights = jax.random.uniform(jax.random.fold_in(jax.random.fold_in(key, 6), dim), (shards_of,), jnp.float32, smallest / len(pieces), high / len(pieces))
        return jnp.repeat(jnp.exp(heights), dims[dim] // shards_of).reshape((-1,) + (1,) * (len(dims) - dim - 1))

    level = one(*pieces[0])
    for cut in pieces[1:]:
        level = level * one(*cut)
    return level


def shared_out(stream_key, own, number, rows, amount, top, bound, lean):
    order = jax.random.permutation(stream_key, amount)
    packed, common = portions_of(amount, rows * top, bound, lean, True), portions_of(amount, rows * top, bound, lean, False)
    places = jnp.arange(amount)

    def named(sizes, turn):
        used = int((sizes > 0).sum())
        fixed = max(1, used // 4)
        moved = fixed + (places - fixed + turn * (used - fixed)) % max(1, amount - fixed)
        return jnp.zeros((amount,), jnp.int32).at[order[jnp.where(places < fixed, places, moved)]].set(jnp.asarray(sizes, jnp.int32))

    sizes = jnp.where(number % 4 == 0, named(packed, number // 4), named(common, number - number // 4 - 1))
    mixed = jax.random.permutation(jax.random.fold_in(own, 3), amount)
    giver, receiver = mixed[0:amount // 2 * 2:2], mixed[1:amount // 2 * 2:2]
    slack = jnp.minimum(sizes[giver] - 1, bound - sizes[receiver]) // 2
    slack = jnp.where((giver == order[0]) | (receiver == order[0]) | (sizes[receiver] == 0), 0, jnp.maximum(slack, 0))
    moved = jax.random.randint(jax.random.fold_in(own, 4), (amount // 2,), 0, 1 << 20) % (slack + 1)
    sizes = sizes.at[giver].add(-moved).at[receiver].add(moved)
    members = jnp.searchsorted(jnp.cumsum(sizes), jnp.arange(rows * top), side="right").astype(jnp.int32)
    grid = members.reshape(top, rows).T
    grid = grid[jax.random.permutation(jax.random.fold_in(own, 1), rows)]
    turn = jax.random.randint(jax.random.fold_in(own, 2), (rows, 1), 0, top)
    return jnp.take_along_axis(grid, (jnp.arange(top)[None, :] + turn) % top, axis=1)


def portions_of(amount, total, bound, lean, full):
    weights = [(1 << 20) // math.isqrt(standing ** lean) + 1 for standing in range(1, amount + 1)]
    largest = bound if full else min(bound, max(-(-total // amount), total * weights[0] // sum(weights)))
    least = 1 if total - largest >= amount - 1 else 0
    holding, surplus = [largest] + [least] * (amount - 1), total - largest - least * (amount - 1)
    while surplus > 0:
        free = [i for i in range(1, amount) if holding[i] < largest] or [i for i in range(1, amount) if holding[i] < bound]
        whole, remaining = sum([weights[i] for i in free]), surplus
        for i in free:
            more = min(bound - holding[i], max(1, remaining * weights[i] // whole), surplus)
            holding[i] = holding[i] + more
            surplus = surplus - more
    return np.array(holding)


def noise(stream_key, extent, deviation, bound, cuts=(), kind=jnp.bfloat16):
    drawn = deviation * jax.random.normal(stream_key, extent, jnp.float32)
    if cuts:
        drawn = drawn * level_of(stream_key, extent, cuts, -0.22, 0.18)
    return jnp.clip(drawn, -bound, bound).astype(kind)


def setup_inputs(seed: int = 0, part: int = 0) -> dict:
    seeds = jax.random.split(jax.random.key(seed), 7)
    part_splits = jax.random.split(jax.random.fold_in(seeds[6], part), 7)
    hidden_slots = noise(part_splits[0], (EXPERTS, N_EXPERT * CAP, FF), 1.0, 6.0, ((0, 16),))
    adapter_in = draw_adapter_in(jax.random.fold_in(seeds[6], 71), part)
    adapter_out = draw_adapter_out(jax.random.fold_in(seeds[6], 71), part)
    expert_ids_keys = jax.random.split(jax.random.fold_in(part_splits[3], 1), TOKENS // TOK_DEV)
    expert_ids_turns = jax.random.permutation(jax.random.fold_in(part_splits[3], 3), TOKENS // TOK_DEV)
    expert_ids = jax.vmap(lambda own, number: shared_out(jax.random.fold_in(part_splits[3], 2), own, number, TOK_DEV, EXPERTS, TOP, CAP, 2))(expert_ids_keys, expert_ids_turns).reshape((TOKENS, TOP))
    gate_weights = jnp.clip(jnp.exp(math.log(0.5) - 2.3025851 * jax.random.uniform(part_splits[4], (TOKENS, TOP), jnp.float32) ** level_of(part_splits[4], (TOKENS, TOP), ((0, 16),), -0.2, 0.2)), 0.05, 0.5)
    cotangent = noise(part_splits[5], (TOKENS, D), 1.0, 6.0, ((0, 16),))
    return dict(hidden_slots=hidden_slots, adapter_in=adapter_in, adapter_out=adapter_out, expert_ids=expert_ids, gate_weights=gate_weights, cotangent=cotangent)


def solve_damped(gram, damp, rhs):
    identity = jnp.eye(gram.shape[0], dtype=jnp.float32)
    factor = jnp.linalg.cholesky(gram + damp * identity)
    return jax.scipy.linalg.cho_solve((factor, True), rhs)

def reference(hidden_slots, adapter_in, adapter_out, expert_ids, gate_weights, cotangent):
    id_blocks = expert_ids.reshape(N_EXPERT, TOK_DEV, TOP)
    chosen = (id_blocks[:, :, :, None] == jnp.arange(EXPERTS, dtype=jnp.int32)).astype(jnp.int32)
    per_token = jnp.sum(chosen, axis=2)
    before = jnp.cumsum(per_token, axis=1) - per_token
    position = jnp.take_along_axis(before, id_blocks, axis=2).astype(jnp.int32)
    sources = jnp.arange(N_EXPERT, dtype=jnp.int32)[:, None, None]
    slot_row = (sources * CAP + position).reshape(-1)
    token_row = jnp.broadcast_to(sources * TOK_DEV + jnp.arange(TOK_DEV, dtype=jnp.int32)[None, :, None], id_blocks.shape).reshape(-1)
    flat_ids = id_blocks.reshape(-1)
    rounded_gate = lax.optimization_barrier(gate_weights.astype(jnp.bfloat16)).astype(jnp.float32)
    slot_token = jnp.full((EXPERTS, N_EXPERT * CAP), TOKENS, jnp.int32).at[flat_ids, slot_row].set(token_row)
    slot_weight = jnp.zeros((EXPERTS, N_EXPERT * CAP), jnp.float32).at[flat_ids, slot_row].set(rounded_gate.reshape(-1))
    padded = jnp.concatenate([cotangent, jnp.zeros((1, D), cotangent.dtype)], axis=0)

    def per_expert(summed, inputs):
        hidden_rows, in_factor, out_factor, token_of, weight_of = inputs
        low_rank = jnp.dot(hidden_rows.astype(jnp.float32), in_factor.T.astype(jnp.float32), preferred_element_type=jnp.float32).astype(jnp.bfloat16)
        expert_out = lax.optimization_barrier(jnp.dot(low_rank.astype(jnp.float32), out_factor.astype(jnp.float32), preferred_element_type=jnp.float32).astype(jnp.bfloat16))
        summed = summed.at[token_of].add(weight_of[:, None] * expert_out.astype(jnp.float32))
        grad_rows = (weight_of[:, None] * padded[token_of].astype(jnp.float32)).astype(jnp.bfloat16)
        grad_low = jnp.dot(grad_rows.astype(jnp.float32), out_factor.T.astype(jnp.float32), preferred_element_type=jnp.float32).astype(jnp.bfloat16)
        out_grad = jnp.dot(low_rank.T.astype(jnp.float32), grad_rows.astype(jnp.float32), preferred_element_type=jnp.float32)
        in_grad = jnp.dot(grad_low.T.astype(jnp.float32), hidden_rows.astype(jnp.float32), preferred_element_type=jnp.float32)
        return (summed, (in_grad, out_grad))
    initial = jnp.zeros((TOKENS + 1, D), jnp.float32)
    summed, grads = lax.scan(per_expert, initial, (hidden_slots, adapter_in, adapter_out, slot_token, slot_weight))
    in_grad, out_grad = grads
    adapter_delta = summed[:TOKENS].astype(jnp.bfloat16)
    in_wide = adapter_in.astype(jnp.float32)
    out_wide = adapter_out.astype(jnp.float32)
    gram_in = jnp.einsum('erf,eqf->erq', in_wide, in_wide, precision=lax.Precision.HIGHEST)
    gram_out = jnp.einsum('erf,eqf->erq', out_wide, out_wide, precision=lax.Precision.HIGHEST)
    damp_in = jnp.sum(jnp.trace(gram_in, axis1=1, axis2=2)) / (R * EXPERTS)
    damp_out = jnp.sum(jnp.trace(gram_out, axis1=1, axis2=2)) / (R * EXPERTS)
    scaled_in_grad = jax.vmap(solve_damped, in_axes=(0, None, 0))(gram_out, damp_out, in_grad)
    scaled_out_grad = jax.vmap(solve_damped, in_axes=(0, None, 0))(gram_in, damp_in, out_grad)
    return (adapter_delta, scaled_in_grad, scaled_out_grad)
```

```python
import functools

import jax
import jax.numpy as jnp
from jax import lax
from jax.experimental import pallas as pl
from jax.experimental.pallas import tpu as pltpu
from jax.sharding import Mesh, PartitionSpec as P

PLANE = 4
BF = jnp.bfloat16
F32 = jnp.float32
HIGHEST = lax.Precision.HIGHEST
PARAMS = pltpu.CompilerParams(vmem_limit_bytes=48 * 1024 * 1024)


def mm(a, b, ca=1, cb=0, precision=None):
    return lax.dot_general(
        a, b, (((ca,), (cb,)), ((), ())), preferred_element_type=F32, precision=precision
    )


def call(kernel, outs, args, flops=0):
    size = sum(x.size * x.dtype.itemsize for x in args)
    size += sum(o.size * o.dtype.itemsize for o in outs)
    return pl.pallas_call(
        kernel,
        out_shape=outs,
        compiler_params=PARAMS,
        cost_estimate=pl.CostEstimate(flops=flops, bytes_accessed=size, transcendentals=0),
    )(*args)


def split(x):
    high = x.astype(BF)
    return high, (x - high.astype(F32)).astype(BF)


def split_factor_kernel(a_out, out):
    width = out.shape[2]
    for q in range(PLANE):
        out[q] = a_out[:, q * width : (q + 1) * width]


def pack_tokens_kernel(cot, ids, gates, out):
    tokens, width = cot.shape[0], out.shape[2]
    for q in range(PLANE):
        out[q, 0:tokens, :] = cot[:, q * width : (q + 1) * width]
    diagonal = (
        lax.broadcasted_iota(jnp.int32, (tokens, tokens), 0)
        == lax.broadcasted_iota(jnp.int32, (tokens, tokens), 1)
    ).astype(BF)
    id_rows = mm(ids[...].astype(F32).astype(BF), diagonal, 0, 0)
    gate_rows = mm(gates[...].astype(BF), diagonal, 0, 0)
    row = lax.broadcasted_iota(jnp.int32, (16, tokens), 0)
    meta = jnp.where(row == 0, id_rows[0:1], 0.0)
    meta = jnp.where(row == 1, id_rows[1:2], meta)
    meta = jnp.where(row == 2, gate_rows[0:1], meta)
    meta = jnp.where(row == 3, gate_rows[1:2], meta).astype(BF)
    for q in range(PLANE):
        out[q, tokens : tokens + 16, 0:tokens] = meta
        out[q, tokens : tokens + 16, tokens:] = jnp.zeros((16, width - tokens), BF)


def low_rank_kernel(hidden, a_in, a_out, out):
    slots = out.shape[2]
    low = mm(a_in[...], hidden[...], 1, 1).astype(BF)
    wide_in, wide_out = a_in[...].astype(F32), a_out[...].astype(F32)
    total_in = jnp.sum(jnp.sum(wide_in * wide_in, axis=1, keepdims=True), axis=0, keepdims=True)
    total_out = jnp.sum(jnp.sum(wide_out * wide_out, axis=1, keepdims=True), axis=0, keepdims=True)
    row = lax.broadcasted_iota(jnp.int32, (16, slots), 0)
    stats = jnp.zeros((16, slots), F32)
    for base, total in ((0, total_in), (3, total_out)):
        rest = jnp.broadcast_to(total, (16, slots))
        for piece in range(3):
            part = rest.astype(BF).astype(F32)
            stats = jnp.where(row == base + piece, part, stats)
            rest = rest - part
    stats = stats.astype(BF)
    for device in range(out.shape[0]):
        plane = device // PLANE
        out[device, 0:16, :] = low[:, plane * slots : (plane + 1) * slots]
        out[device, 16:32, :] = stats


def fold_of(slots, experts, capacity, source):
    column = lax.broadcasted_iota(jnp.int32, (slots, experts * capacity), 1)
    row = lax.broadcasted_iota(jnp.int32, (slots, experts * capacity), 0)
    return (row == source * capacity + lax.rem(column, capacity)).astype(BF)


def own_expert(experts, capacity, rank):
    shape = (experts * rank, experts * capacity)
    row = lax.div(lax.broadcasted_iota(jnp.int32, shape, 0), rank)
    column = lax.div(lax.broadcasted_iota(jnp.int32, shape, 1), capacity)
    return row == column


def weighted_rows_kernel(packed, lows, z_out, w_out, part_out):
    experts, slots = lows.shape[0], lows.shape[2]
    rank, capacity = 16, slots // PLANE
    tokens = packed.shape[1] - 16
    low = lows[:, 0:rank, :].reshape(experts * rank, slots)
    own = own_expert(experts, capacity, rank)
    expert = lax.broadcasted_iota(jnp.int32, (experts, tokens), 0).astype(F32)
    earlier = (
        lax.broadcasted_iota(jnp.int32, (tokens, tokens), 0)
        < lax.broadcasted_iota(jnp.int32, (tokens, tokens), 1)
    ).astype(BF)
    place = lax.broadcasted_iota(jnp.int32, (experts, capacity, tokens), 1).astype(F32)
    part = jnp.zeros(part_out.shape, F32)
    for s in range(PLANE):
        meta = packed[s, tokens : tokens + 16, 0:tokens].astype(F32)
        first = (meta[0:1] == expert).astype(F32)
        second = (meta[1:2] == expert).astype(F32)
        before = mm((first + second).astype(BF), earlier)
        gate = first * meta[2:3] + second * meta[3:4]
        spread = jnp.where(before[:, None, :] == place, gate[:, None, :], 0.0)
        weights = spread.reshape(experts * capacity, tokens).astype(BF)
        wide = mm(low, fold_of(slots, experts, capacity, s))
        wide = jnp.where(own, wide, 0.0).astype(BF)
        z = mm(wide, weights).astype(BF)
        z_out[:, s * tokens : (s + 1) * tokens] = z
        w_out[s] = weights
        part = part + mm(z, packed[s, 0:tokens, :])
    part_out[...] = part.astype(BF)


def grad_low_kernel(packed, factor, w, out):
    experts = factor.shape[0] // 16
    slots, tokens = out.shape[1], w.shape[2]
    capacity = slots // PLANE
    own = own_expert(experts, capacity, 16)
    total = jnp.zeros(out.shape, F32)
    for s in range(PLANE):
        coords = mm(factor[...], packed[s, 0:tokens, :], 1, 1)
        high, low = split(coords)
        picked = mm(high, w[s], 1, 1) + mm(low, w[s], 1, 1)
        picked = jnp.where(own, picked, 0.0)
        high, low = split(picked)
        fold = fold_of(slots, experts, capacity, s)
        total = total + mm(high, fold, 1, 1) + mm(low, fold, 1, 1)
    out[...] = total


def delta_kernel(z, factor, out):
    tokens = out.shape[1]
    for s in range(PLANE):
        rows = mm(z[:, s * tokens : (s + 1) * tokens], factor[...], 0, 0)
        out[s] = rows.astype(BF)


def inverse_kernel(a_in, a_out, lows, inv_in, inv_out):
    experts = lows.shape[0]
    stats = jnp.sum(lows[:, 16:32, :].astype(F32), axis=0)
    row = lax.broadcasted_iota(jnp.int32, (16, 16), 0)
    column = lax.broadcasted_iota(jnp.int32, (16, 16), 1)
    eye = (row == column).astype(F32)
    works = []
    for base, factor in ((0, a_in), (3, a_out)):
        pieces = stats[base : base + 1, 0:1] + stats[base + 1 : base + 2, 0:1]
        damp = (pieces + stats[base + 2 : base + 3, 0:1]) / (16.0 * experts)
        gram = mm(factor[...], factor[...], 1, 1) + damp * eye
        works.append([gram, eye])
    for j in range(16):
        for work in works:
            gram, inverse = work
            pivot = 1.0 / gram[j : j + 1, j : j + 1]
            gram_row, inverse_row = gram[j : j + 1] * pivot, inverse[j : j + 1] * pivot
            scale = gram[:, j : j + 1]
            work[0] = jnp.where(row == j, gram_row, gram - scale * gram_row)
            work[1] = jnp.where(row == j, inverse_row, inverse - scale * inverse_row)
    inv_in[...] = works[0][1]
    inv_out[...] = works[1][1]


def scaled_in_kernel(coords, hidden, inverse, out):
    planes = coords.shape[0] // PLANE
    pieces = []
    for z in range(planes):
        total = coords[PLANE * z]
        for q in range(1, PLANE):
            total = total + coords[PLANE * z + q]
        pieces.append(total)
    grad_low = jnp.concatenate(pieces, axis=1).astype(BF)
    out[...] = mm(inverse[...], mm(grad_low, hidden[...]), precision=HIGHEST)


def scaled_out_kernel(rows, inverse, out):
    width = rows.shape[2]
    for q in range(PLANE):
        out[:, q * width : (q + 1) * width] = mm(inverse[...], rows[q], precision=HIGHEST)


def on_device(hidden_slots, adapter_in, adapter_out, expert_ids, gate_weights, cotangent):
    planes = lax.axis_size("z")
    experts = planes * PLANE
    hidden, a_in, a_out = hidden_slots[0], adapter_in[0], adapter_out[0]
    rank, width = a_out.shape
    quarter = width // PLANE
    tokens = cotangent.shape[0]
    slots = hidden.shape[0] // planes
    capacity = slots // PLANE
    struct = jax.ShapeDtypeStruct
    plane, every = ("y", "core"), ("z", "y", "core")
    exchange = functools.partial(lax.all_to_all, split_axis=0, concat_axis=0, tiled=True)

    (own_factor,) = call(split_factor_kernel, [struct((PLANE, rank, quarter), BF)], [a_out])
    plane_factor = exchange(own_factor, plane).reshape(PLANE * rank, quarter)
    factor = lax.all_gather(plane_factor, "z", axis=0, tiled=True)

    (packed,) = call(
        pack_tokens_kernel,
        [struct((PLANE, tokens + 16, quarter), BF)],
        [cotangent, expert_ids, gate_weights],
    )
    packed = exchange(packed, plane)

    (lows,) = call(
        low_rank_kernel, [struct((experts, 2 * rank, slots), BF)], [hidden, a_in, a_out]
    )
    lows = exchange(lows, every)

    inv_in, inv_out = call(
        inverse_kernel, [struct((rank, rank), F32)] * 2, [a_in, a_out, lows]
    )
    z, weights, part = call(
        weighted_rows_kernel,
        [
            struct((experts * rank, PLANE * tokens), BF),
            struct((PLANE, experts * capacity, tokens), BF),
            struct((experts * rank, quarter), BF),
        ],
        [packed, lows],
    )
    part = exchange(part.reshape(planes, PLANE * rank, quarter), "z")
    rows = jnp.sum(part.astype(F32), axis=0).reshape(PLANE, rank, quarter)
    rows = exchange(rows, plane)
    (scaled_out,) = call(scaled_out_kernel, [struct((rank, width), F32)], [rows, inv_in])

    (coords,) = call(
        grad_low_kernel, [struct((experts * rank, slots), F32)], [packed, factor, weights]
    )
    coords = exchange(coords.reshape(experts, rank, slots), every)
    (scaled_in,) = call(
        scaled_in_kernel, [struct((rank, hidden.shape[1]), F32)], [coords, hidden, inv_out]
    )

    (delta,) = call(delta_kernel, [struct((PLANE, tokens, quarter), BF)], [z, factor])
    delta = exchange(delta, plane)
    delta = jnp.swapaxes(delta, 0, 1).reshape(tokens, width)
    return delta, scaled_in[None], scaled_out[None]


def solution(mesh):
    groups, experts = mesh.shape["group"], mesh.shape["expert"]
    fine = Mesh(
        mesh.devices.reshape(groups, experts // PLANE, PLANE // 2, 2),
        ("group", "z", "y", "core"),
    )
    every = ("z", "y", "core")
    return jax.shard_map(
        on_device,
        mesh=fine,
        in_specs=(
            P(("group", *every), None, None),
            P(every, None, None),
            P(every, None, None),
            P(("group", *every), None),
            P(("group", *every), None),
            P(("group", *every), None),
        ),
        out_specs=(
            P(("group", *every), None),
            P(("group", *every), None, None),
            P(("group", *every), None, None),
        ),
        check_vma=False,
    )
```

```python
import jax
import jax.numpy as jnp
from jax import lax
from jax.experimental import pallas as pl
from jax.experimental.pallas import tpu as pltpu
from jax.sharding import PartitionSpec as P

BF = jnp.bfloat16
F32 = jnp.float32
HIGHEST = lax.Precision.HIGHEST
RANK = 16
CHUNKS = 2


def mm(a, b, ca=1, cb=0, precision=None):
    return lax.dot_general(
        a, b, (((ca,), (cb,)), ((), ())), preferred_element_type=F32, precision=precision
    )


def call(kernel, outs, args, scalars=None, flops=0):
    size = sum(x.size * x.dtype.itemsize for x in args)
    size += sum(o.size * o.dtype.itemsize for o in outs)
    specs = [pl.BlockSpec(memory_space=pltpu.VMEM)] * len(args)
    if scalars is not None:
        args = [scalars, *args]
        specs = [pl.BlockSpec(memory_space=pltpu.SMEM), *specs]
    return pl.pallas_call(
        kernel,
        out_shape=[jax.ShapeDtypeStruct(o.shape, o.dtype) for o in outs],
        in_specs=specs,
        out_specs=[pl.BlockSpec(memory_space=pltpu.VMEM)] * len(outs),
        compiler_params=pltpu.CompilerParams(vmem_limit_bytes=48 * 1024 * 1024),
        cost_estimate=pl.CostEstimate(flops=flops, bytes_accessed=size, transcendentals=0),
    )(*args)


def split(x):
    high = x.astype(BF)
    return high, (x - high.astype(F32)).astype(BF)


def lanes(start, size):
    return pl.ds(pl.multiple_of(start, 128), size)


def half_factor_kernel(where, a_out, out):
    half = out.shape[1]
    out[...] = a_out[:, lanes(where[2] * half, half)]


def pack_tokens_kernel(where, cot, ids, gates, out, own):
    tokens, half = cot.shape[0], out.shape[1]
    out[0:tokens, :] = cot[:, lanes((1 - where[1]) * half, half)]
    diagonal = (
        lax.broadcasted_iota(jnp.int32, (tokens, tokens), 0)
        == lax.broadcasted_iota(jnp.int32, (tokens, tokens), 1)
    ).astype(BF)
    id_rows = mm(ids[...].astype(F32).astype(BF), diagonal, 0, 0)
    gate_rows = mm(gates[...].astype(BF), diagonal, 0, 0)
    row = lax.broadcasted_iota(jnp.int32, (16, tokens), 0)
    meta = jnp.where(row == 0, id_rows[0:1], 0.0)
    meta = jnp.where(row == 1, id_rows[1:2], meta)
    meta = jnp.where(row == 2, gate_rows[0:1], meta)
    meta = jnp.where(row == 3, gate_rows[1:2], meta).astype(BF)
    own[...] = meta
    out[tokens : tokens + 16, 0:tokens] = meta
    out[tokens : tokens + 16, tokens:] = jnp.zeros((16, half - tokens), BF)


def low_rank_kernel(hidden, a_in, a_out, out):
    slots = out.shape[2] // 2
    low = mm(a_in[...], hidden[...], 1, 1).astype(BF)
    wide_in, wide_out = a_in[...].astype(F32), a_out[...].astype(F32)
    total_in = jnp.sum(jnp.sum(wide_in * wide_in, axis=1, keepdims=True), axis=0, keepdims=True)
    total_out = jnp.sum(jnp.sum(wide_out * wide_out, axis=1, keepdims=True), axis=0, keepdims=True)
    row = lax.broadcasted_iota(jnp.int32, (RANK, slots), 0)
    stats = jnp.zeros((RANK, slots), F32)
    for base, total in ((0, total_in), (3, total_out)):
        rest = jnp.broadcast_to(total, (RANK, slots))
        for piece in range(3):
            part = rest.astype(BF).astype(F32)
            stats = jnp.where(row == base + piece, part, stats)
            rest = rest - part
    stats = stats.astype(BF)
    for device in range(out.shape[0]):
        chip = device // 2
        out[device, :, 0:slots] = low[:, chip * slots : (chip + 1) * slots]
        out[device, :, slots:] = stats


def fold_of(slots, experts, capacity, source):
    column = lax.broadcasted_iota(jnp.int32, (slots, experts * capacity), 1)
    row = lax.broadcasted_iota(jnp.int32, (slots, experts * capacity), 0)
    return (row == source * capacity + lax.rem(column, capacity)).astype(BF)


def own_expert(experts, capacity):
    shape = (experts * RANK, experts * capacity)
    row = lax.div(lax.broadcasted_iota(jnp.int32, shape, 0), RANK)
    column = lax.div(lax.broadcasted_iota(jnp.int32, shape, 1), capacity)
    return row == column


def relative_experts(order_size, tokens, me):
    row = lax.broadcasted_iota(jnp.int32, (order_size, tokens), 0)
    return jnp.bitwise_xor(row, me).astype(F32)


def partial_kernel(order, where, cot, packed, own_meta, lows, z_out, w_out, *outs):
    keeps, sends = outs[:CHUNKS], outs[CHUNKS:]
    me, core = where[0], where[1]
    experts, tokens = lows.shape[0], cot.shape[0]
    slots = lows.shape[2] // 2
    capacity = slots // 2
    half = packed.shape[1]
    low = jnp.concatenate(
        [lows[jnp.bitwise_xor(me, e)][:, 0:slots] for e in range(experts)], axis=0
    )
    own = own_expert(experts, capacity)
    expert = relative_experts(experts, tokens, me)
    earlier = (
        lax.broadcasted_iota(jnp.int32, (tokens, tokens), 0)
        < lax.broadcasted_iota(jnp.int32, (tokens, tokens), 1)
    ).astype(BF)
    place = lax.broadcasted_iota(jnp.int32, (experts, capacity, tokens), 1).astype(F32)
    rows = []
    for s in range(2):
        meta = (own_meta[...] if s == 0 else packed[tokens:, 0:tokens]).astype(F32)
        first = (meta[0:1] == expert).astype(F32)
        second = (meta[1:2] == expert).astype(F32)
        before = mm((first + second).astype(BF), earlier)
        gate = first * meta[2:3] + second * meta[3:4]
        spread = jnp.where(before[:, None, :] == place, gate[:, None, :], 0.0)
        weights = spread.reshape(experts * capacity, tokens).astype(BF)
        source = jnp.bitwise_xor(core, s)
        wide = mm(low, fold_of(slots, experts, capacity, source))
        wide = jnp.where(own, wide, 0.0).astype(BF)
        z = mm(wide, weights).astype(BF)
        rows.append(z.reshape(experts // 4, 2, 2 * RANK, tokens))
        if s == 0:
            w_out[...] = weights
            for place_of, e in enumerate(order):
                z_out[place_of * RANK : (place_of + 1) * RANK, :] = z[e * RANK : (e + 1) * RANK]
    count = experts * RANK // 2
    wide = half // CHUNKS
    for piece in range(CHUNKS):
        mine = cot[:, lanes(core * half + piece * wide, wide)]
        other = packed[0:tokens, piece * wide : (piece + 1) * wide]
        for side, target in ((0, keeps[piece]), (1, sends[piece])):
            first = rows[0][:, side].reshape(count, tokens)
            second = rows[1][:, side].reshape(count, tokens)
            target[...] = (mm(first, mine) + mm(second, other)).astype(target.dtype)


def fold_step_kernel(keep, received, kept, sent):
    rows, width = keep.shape
    total = keep[...] + received[...].astype(F32)
    total = total.reshape(rows // (4 * RANK), 2, 2 * RANK, width)
    kept[...] = total[:, 0].reshape(rows // 2, width)
    sent[...] = total[:, 1].reshape(rows // 2, width).astype(sent.dtype)


def last_fold_kernel(keep, received, kept, sent):
    total = keep[...] + received[...].astype(F32)
    kept[...] = total[0:RANK]
    sent[...] = total[RANK:]


def grad_low_kernel(order, where, cot, w, *refs):
    factors, out = refs[:-1], refs[-1]
    me, side = where[0], where[2]
    experts, _, slots = out.shape
    tokens, half = cot.shape[0], factors[0].shape[1]
    capacity = slots // 4
    own_side = cot[:, lanes(side * half, half)]
    far_side = cot[:, lanes((1 - side) * half, half)]
    blocks = []
    for near, far in zip(factors[0::2], factors[1::2]):
        rows = mm(near[...], own_side, 1, 1) + mm(far[...], far_side, 1, 1)
        blocks += [rows[r : r + RANK] for r in range(0, rows.shape[0], RANK)]
    coords = jnp.concatenate([blocks[order.index(e)] for e in range(experts)], axis=0)
    high, low = split(coords)
    picked = mm(high, w[...], 1, 1) + mm(low, w[...], 1, 1)
    picked = jnp.where(own_expert(experts, capacity), picked, 0.0).astype(BF)
    fold = fold_of(slots, experts, capacity, lax.rem(me, 4))
    rows = mm(picked, fold, 1, 1).astype(out.dtype)
    for e in range(experts):
        out[jnp.bitwise_xor(me, e)] = rows[e * RANK : (e + 1) * RANK]


def delta_kernel(where, z, *refs):
    factors, out = refs[:-1], refs[-1]
    half = factors[0].shape[1]
    for flip in range(2):
        total, start = None, 0
        for factor in factors[flip::2]:
            part = mm(z[start : start + factor.shape[0], :], factor[...], 0, 0)
            total = part if total is None else total + part
            start += factor.shape[0]
        side = jnp.bitwise_xor(where[2], flip)
        out[:, lanes(side * half, half)] = total.astype(BF)


def inverse_kernel(a_in, a_out, lows, inv_in, inv_out):
    experts, _, double = lows.shape
    stats = jnp.sum(lows[:, :, double // 2 :].astype(F32), axis=0)
    row = lax.broadcasted_iota(jnp.int32, (RANK, RANK), 0)
    column = lax.broadcasted_iota(jnp.int32, (RANK, RANK), 1)
    eye = (row == column).astype(F32)
    works = []
    for base, factor in ((0, a_in), (3, a_out)):
        pieces = stats[base : base + 1, 0:1] + stats[base + 1 : base + 2, 0:1]
        damp = (pieces + stats[base + 2 : base + 3, 0:1]) / (float(RANK) * experts)
        gram = mm(factor[...], factor[...], 1, 1) + damp * eye
        works.append([gram, eye])
    for j in range(RANK):
        for work in works:
            gram, inverse = work
            pivot = 1.0 / gram[j : j + 1, j : j + 1]
            gram_row, inverse_row = gram[j : j + 1] * pivot, inverse[j : j + 1] * pivot
            scale = gram[:, j : j + 1]
            work[0] = jnp.where(row == j, gram_row, gram - scale * gram_row)
            work[1] = jnp.where(row == j, inverse_row, inverse - scale * inverse_row)
    inv_in[...] = works[0][1]
    inv_out[...] = works[1][1]


def scaled_in_kernel(coords, hidden, inverse, out):
    pieces = []
    for base in range(0, coords.shape[0], 4):
        total = coords[base].astype(F32)
        for q in range(1, 4):
            total = total + coords[base + q].astype(F32)
        pieces.append(total)
    grad_low = jnp.concatenate(pieces, axis=1).astype(BF)
    out[...] = mm(inverse[...], mm(grad_low, hidden[...]), precision=HIGHEST)


def scaled_out_kernel(where, inverse, *refs):
    pieces, out = refs[:-1], refs[-1]
    wide = pieces[0].shape[1]
    half = wide * CHUNKS
    for flip in range(2):
        base = jnp.bitwise_xor(where[1], flip) * half
        for piece in range(CHUNKS):
            rows = mm(inverse[...], pieces[flip * CHUNKS + piece][...], precision=HIGHEST)
            out[:, lanes(base + piece * wide, wide)] = rows


def on_device(hidden_slots, adapter_in, adapter_out, expert_ids, gate_weights, cotangent):
    experts, groups = lax.axis_size("expert"), lax.axis_size("group")
    me, group = lax.axis_index("expert"), lax.axis_index("group")
    where = jnp.stack([me, me % 2, group % 2]).astype(jnp.int32)
    hidden, a_in, a_out = hidden_slots[0], adapter_in[0], adapter_out[0]
    width = a_out.shape[1]
    half = width // 2
    wide = half // CHUNKS
    tokens = cotangent.shape[0]
    capacity = hidden.shape[0] // experts
    struct = jax.ShapeDtypeStruct

    def swap(x, bit):
        return lax.ppermute(x, "expert", [(i, i ^ bit) for i in range(experts)])

    def swap_side(x):
        return lax.ppermute(x, "group", [(i, i ^ 1) for i in range(groups)])

    def spread(x):
        return lax.all_to_all(x, "expert", split_axis=0, concat_axis=0, tiled=True)

    far_bits = []
    bit = 4
    while bit < experts:
        far_bits.append(bit)
        bit *= 2

    (block,) = call(half_factor_kernel, [struct((RANK, half), BF)], [a_out], where)
    order = [0]
    for bit in [2, *reversed(far_bits)]:
        received = swap(block, bit)
        order = order + [e ^ bit for e in order]
        if bit == far_bits[0]:
            near = [block, received]
        else:
            block = jnp.concatenate([block, received], axis=0)
    order = order + [e ^ 1 for e in order]

    packed, own_meta = call(
        pack_tokens_kernel,
        [struct((tokens + 16, half), BF), struct((16, tokens), BF)],
        [cotangent, expert_ids, gate_weights],
        where,
    )
    packed = swap(packed, 1)
    (lows,) = call(
        low_rank_kernel, [struct((experts, RANK, 4 * capacity), BF)], [hidden, a_in, a_out]
    )
    lows = spread(lows)
    inv_in, inv_out = call(
        inverse_kernel, [struct((RANK, RANK), F32)] * 2, [a_in, a_out, lows]
    )

    count = experts * RANK // 2
    z, weights, *parts = call(
        lambda *refs: partial_kernel(order, *refs),
        [struct((experts * RANK, tokens), BF), struct((experts * capacity, tokens), BF)]
        + [struct((count, wide), F32)] * CHUNKS
        + [struct((count, wide), BF)] * CHUNKS,
        [cotangent, packed, own_meta, lows],
        where,
    )
    kept, sent = parts[:CHUNKS], parts[CHUNKS:]
    own_rows, far_rows = [], []
    for piece in range(CHUNKS):
        keep, send, rows = kept[piece], sent[piece], count
        for bit in [2, *far_bits]:
            received = swap(send, bit)
            if bit == far_bits[-1]:
                shapes, step = [struct((RANK, wide), F32)] * 2, last_fold_kernel
            else:
                rows //= 2
                shapes = [struct((rows, wide), F32), struct((rows, wide), BF)]
                step = fold_step_kernel
            keep, send = call(step, shapes, [keep, received])
        own_rows.append(keep)
        far_rows.append(swap(send, 1))

    factors = []
    for block in near:
        factors += [block, swap_side(block)]
    factors = factors + [swap(block, 1) for block in factors]
    (coords,) = call(
        lambda *refs: grad_low_kernel(order, *refs),
        [struct((experts, RANK, 4 * capacity), BF)],
        [cotangent, weights, *factors],
        where,
    )
    coords = spread(coords)
    (delta,) = call(delta_kernel, [struct((tokens, width), BF)], [z, *factors], where)
    (scaled_in,) = call(
        scaled_in_kernel, [struct((RANK, hidden.shape[1]), F32)], [coords, hidden, inv_out]
    )
    (scaled_out,) = call(
        scaled_out_kernel, [struct((RANK, width), F32)], [inv_in, *own_rows, *far_rows], where
    )
    return delta, scaled_in[None], scaled_out[None]


def solution(mesh):
    every = ("group", "expert")
    return jax.shard_map(
        on_device,
        mesh=mesh,
        in_specs=(
            P(every, None, None),
            P("expert", None, None),
            P("expert", None, None),
            P(every, None),
            P(every, None),
            P(every, None),
        ),
        out_specs=(P(every, None), P(every, None, None), P(every, None, None)),
        check_vma=False,
    )
```

```python
import jax
import jax.numpy as jnp
import numpy as np
from jax import lax
from jax.experimental import pallas as pl
from jax.experimental.pallas import tpu as pltpu
from jax.sharding import PartitionSpec as P

BF = jnp.bfloat16
F32 = jnp.float32
HIGHEST = lax.Precision.HIGHEST
RANK = 16
CHUNKS = 2
MIB = 1024 * 1024


def mm(a, b, ca=1, cb=0, precision=None):
    return lax.dot_general(
        a, b, (((ca,), (cb,)), ((), ())), preferred_element_type=F32, precision=precision
    )


def call(kernel, outs, args, scalars=None, after=(), scratch=(), spaces=None):
    size = sum(x.size * x.dtype.itemsize for x in [*args, *outs])
    total = size + sum(np.prod(x.shape) * x.dtype.itemsize for x in scratch if len(getattr(x, "shape", ())) > 1)
    spaces = spaces or [pltpu.VMEM] * len(args)
    specs = [pl.BlockSpec(memory_space=space) for space in spaces]
    if scalars is not None:
        args = [scalars, *args]
        specs = [pl.BlockSpec(memory_space=pltpu.SMEM), *specs]
    used = len(args)

    def body(*refs):
        kernel(*refs[:used], *refs[used + len(after) :])

    return pl.pallas_call(
        body,
        out_shape=[jax.ShapeDtypeStruct(o.shape, o.dtype) for o in outs],
        in_specs=specs + [pl.BlockSpec(memory_space=pl.ANY)] * len(after),
        out_specs=[pl.BlockSpec(memory_space=pltpu.VMEM)] * len(outs),
        scratch_shapes=list(scratch),
        compiler_params=pltpu.CompilerParams(
            vmem_limit_bytes=min(60 * MIB, int(8 * MIB + 1.5 * total))
        ),
        cost_estimate=pl.CostEstimate(flops=0, bytes_accessed=size, transcendentals=0),
    )(*args, *after)


def split(x):
    high = x.astype(BF)
    return high, (x - high.astype(F32)).astype(BF)


def lanes(start, size):
    return pl.ds(pl.multiple_of(start, 128), size)


def half_factor_kernel(where, a_out, out, sem):
    half = out.shape[1]
    copy = pltpu.make_async_copy(a_out.at[:, lanes(where[2] * half, half)], out, sem)
    copy.start()
    copy.wait()


def pack_tokens_kernel(where, cot, ids, gates, out, own, sem):
    tokens, half = cot.shape[0], out.shape[1]
    far = lanes((1 - where[1]) * half, half)
    copy = pltpu.make_async_copy(cot.at[:, far], out.at[0:tokens, :], sem)
    copy.start()
    row = lax.broadcasted_iota(jnp.int32, (16, tokens), 0)
    id_rows, gate_rows = ids[...].astype(F32), gates[...].astype(BF).astype(F32)
    meta = jnp.where(row == 0, id_rows[0:1], 0.0)
    meta = jnp.where(row == 1, id_rows[1:2], meta)
    meta = jnp.where(row == 2, gate_rows[0:1], meta)
    meta = jnp.where(row == 3, gate_rows[1:2], meta).astype(BF)
    own[...] = meta
    out[tokens : tokens + 16, 0:tokens] = meta
    out[tokens : tokens + 16, tokens:] = jnp.zeros((16, half - tokens), BF)
    copy.wait()


def low_rank_kernel(hidden, a_in, a_out, low, stats_out, rows, sem):
    copy = pltpu.make_async_copy(hidden, rows, sem)
    copy.start()
    wide_in, wide_out = a_in[...].astype(F32), a_out[...].astype(F32)
    total_in = jnp.sum(jnp.sum(wide_in * wide_in, axis=1, keepdims=True), axis=0, keepdims=True)
    total_out = jnp.sum(jnp.sum(wide_out * wide_out, axis=1, keepdims=True), axis=0, keepdims=True)
    row = lax.broadcasted_iota(jnp.int32, stats_out.shape, 0)
    stats = jnp.zeros(stats_out.shape, F32)
    for base, total in ((0, total_in), (3, total_out)):
        rest = jnp.broadcast_to(total, stats_out.shape)
        for piece in range(3):
            part = rest.astype(BF).astype(F32)
            stats = jnp.where(row == base + piece, part, stats)
            rest = rest - part
    stats_out[...] = stats.astype(BF)
    copy.wait()
    low[...] = mm(a_in[...], rows[...], 1, 1).astype(BF)


def pack_low_kernel(low, stats, out):
    slots = out.shape[2] // 2
    for device in range(out.shape[0]):
        chip = device // 2
        out[device, :, 0:slots] = low[:, chip * slots : (chip + 1) * slots]
        out[device, :, slots:] = stats[...]


def join_kernel(first, second, out):
    rows = first.shape[0]
    out[0:rows, :] = first[...]
    out[rows:, :] = second[...]


def fold_of(slots, experts, capacity, source):
    column = lax.broadcasted_iota(jnp.int32, (slots, experts * capacity), 1)
    row = lax.broadcasted_iota(jnp.int32, (slots, experts * capacity), 0)
    return (row == source * capacity + lax.rem(column, capacity)).astype(BF)


def own_expert(experts, capacity):
    shape = (experts * RANK, experts * capacity)
    row = lax.div(lax.broadcasted_iota(jnp.int32, shape, 0), RANK)
    column = lax.div(lax.broadcasted_iota(jnp.int32, shape, 1), capacity)
    return row == column


def relative_experts(order_size, tokens, me):
    row = lax.broadcasted_iota(jnp.int32, (order_size, tokens), 0)
    return jnp.bitwise_xor(row, me).astype(F32)


def partial_kernel(order, where, cot, packed, own_meta, lows, z_out, w_out, *outs):
    keeps, sends = outs[:CHUNKS], outs[CHUNKS:]
    me, core = where[0], where[1]
    experts, tokens = lows.shape[0], cot.shape[0]
    slots = lows.shape[2] // 2
    capacity = slots // 2
    half = packed.shape[1]
    low = jnp.concatenate(
        [lows[jnp.bitwise_xor(me, e)][:, 0:slots] for e in range(experts)], axis=0
    )
    own = own_expert(experts, capacity)
    expert = relative_experts(experts, tokens, me)
    earlier = (
        lax.broadcasted_iota(jnp.int32, (tokens, tokens), 0)
        < lax.broadcasted_iota(jnp.int32, (tokens, tokens), 1)
    ).astype(BF)
    place = lax.broadcasted_iota(jnp.int32, (experts, capacity, tokens), 1).astype(F32)
    rows = []
    for s in range(2):
        meta = (own_meta[...] if s == 0 else packed[tokens:, 0:tokens]).astype(F32)
        first = (meta[0:1] == expert).astype(F32)
        second = (meta[1:2] == expert).astype(F32)
        before = mm((first + second).astype(BF), earlier)
        gate = first * meta[2:3] + second * meta[3:4]
        spread = jnp.where(before[:, None, :] == place, gate[:, None, :], 0.0)
        weights = spread.reshape(experts * capacity, tokens).astype(BF)
        source = jnp.bitwise_xor(core, s)
        wide = mm(low, fold_of(slots, experts, capacity, source))
        wide = jnp.where(own, wide, 0.0).astype(BF)
        exact = mm(wide, weights)
        z = exact.astype(BF)
        rows.append(z.reshape(experts // 4, 2, 2 * RANK, tokens))
        if s == 0:
            w_out[...] = weights
            ordered = jnp.concatenate([exact[e * RANK : (e + 1) * RANK] for e in order], axis=0)
            z_out[...] = ordered.T.astype(BF)
    count = experts * RANK // 2
    wide = half // CHUNKS
    for piece in range(CHUNKS):
        mine = cot[:, lanes(core * half + piece * wide, wide)]
        other = packed[0:tokens, piece * wide : (piece + 1) * wide]
        for side, target in ((0, keeps[piece]), (1, sends[piece])):
            first = rows[0][:, side].reshape(count, tokens)
            second = rows[1][:, side].reshape(count, tokens)
            target[...] = (mm(first, mine) + mm(second, other)).astype(target.dtype)


def fold_step_kernel(keep, received, kept, sent):
    rows, width = keep.shape
    total = keep[...] + received[...].astype(F32)
    total = total.reshape(rows // (4 * RANK), 2, 2 * RANK, width)
    kept[...] = total[:, 0].reshape(rows // 2, width)
    sent[...] = total[:, 1].reshape(rows // 2, width).astype(sent.dtype)


def last_fold_kernel(keep, received, kept, sent):
    total = keep[...] + received[...].astype(F32)
    kept[...] = total[0:RANK]
    sent[...] = total[RANK:]


def factor_kernel(order, where, cot, w, z, *refs):
    count = len(order) * RANK
    pieces = 8
    factors, (coords_out, delta, tokens_in, table, sems) = refs[:pieces], refs[pieces:]
    me, side = where[0], where[2]
    experts, _, slots = coords_out.shape
    tokens, half = cot.shape[0], factors[0].shape[1]
    capacity = slots // 4
    copies = [pltpu.make_async_copy(cot, tokens_in, sems.at[pieces])]
    for flip in range(2):
        start = 0
        for i, factor in enumerate(factors[flip::2]):
            size = factor.shape[0]
            target = table.at[flip, start : start + size, :]
            copies.append(pltpu.make_async_copy(factor, target, sems.at[4 * flip + i]))
            start += size
    for copy in copies:
        copy.start()
    for copy in copies[:5]:
        copy.wait()
    cut = half // 4
    coords = jnp.zeros((count, tokens), F32)
    for flip in range(2):
        if flip == 1:
            for copy in copies[5:]:
                copy.wait()
        base = jnp.bitwise_xor(side, flip) * half
        for piece in range(4):
            block = table[flip, :, piece * cut : (piece + 1) * cut]
            here = lanes(base + piece * cut, cut)
            delta[:, here] = mm(z[...], block).astype(BF)
            coords = coords + mm(block, tokens_in[:, here], 1, 1)
    blocks = [order.index(e) * RANK for e in range(experts)]
    coords = jnp.concatenate([coords[b : b + RANK] for b in blocks], axis=0)
    high, low = split(coords)
    picked = mm(high, w[...], 1, 1) + mm(low, w[...], 1, 1)
    picked = jnp.where(own_expert(experts, capacity), picked, 0.0).astype(BF)
    fold = fold_of(slots, experts, capacity, lax.rem(me, 4))
    rows = mm(picked, fold, 1, 1).astype(coords_out.dtype)
    for e in range(experts):
        coords_out[jnp.bitwise_xor(me, e)] = rows[e * RANK : (e + 1) * RANK]


def inverse_kernel(a_in, a_out, lows, inv_in, inv_out):
    experts, _, double = lows.shape
    stats = jnp.sum(lows[:, :, double // 2 :].astype(F32), axis=0)
    row = lax.broadcasted_iota(jnp.int32, (RANK, RANK), 0)
    column = lax.broadcasted_iota(jnp.int32, (RANK, RANK), 1)
    eye = (row == column).astype(F32)
    works = []
    for base, factor in ((0, a_in), (3, a_out)):
        pieces = stats[base : base + 1, 0:1] + stats[base + 1 : base + 2, 0:1]
        damp = (pieces + stats[base + 2 : base + 3, 0:1]) / (float(RANK) * experts)
        gram = mm(factor[...], factor[...], 1, 1) + damp * eye
        works.append([gram, eye])
    for j in range(RANK):
        for work in works:
            gram, inverse = work
            pivot = 1.0 / gram[j : j + 1, j : j + 1]
            gram_row, inverse_row = gram[j : j + 1] * pivot, inverse[j : j + 1] * pivot
            scale = gram[:, j : j + 1]
            work[0] = jnp.where(row == j, gram_row, gram - scale * gram_row)
            work[1] = jnp.where(row == j, inverse_row, inverse - scale * inverse_row)
    inv_in[...] = works[0][1]
    inv_out[...] = works[1][1]


def scaled_in_kernel(coords, hidden, inverse, out):
    pieces = []
    for base in range(0, coords.shape[0], 4):
        total = coords[base].astype(F32)
        for q in range(1, 4):
            total = total + coords[base + q].astype(F32)
        pieces.append(total)
    grad_low = jnp.concatenate(pieces, axis=1).astype(BF)
    out[...] = mm(inverse[...], mm(grad_low, hidden[...]), precision=HIGHEST)


def scaled_out_kernel(where, inverse, *refs):
    pieces, out = refs[:-1], refs[-1]
    wide = pieces[0].shape[1]
    half = wide * CHUNKS
    for flip in range(2):
        base = jnp.bitwise_xor(where[1], flip) * half
        for piece in range(CHUNKS):
            rows = mm(inverse[...], pieces[flip * CHUNKS + piece][...], precision=HIGHEST)
            out[:, lanes(base + piece * wide, wide)] = rows


def relative_order(far_bits):
    order = [0]
    for bit in [2, *reversed(far_bits), 1]:
        order = order + [e ^ bit for e in order]
    return order


def on_device(hidden_slots, adapter_in, adapter_out, expert_ids, gate_weights, cotangent):
    experts, groups = lax.axis_size("expert"), lax.axis_size("group")
    me, group = lax.axis_index("expert"), lax.axis_index("group")
    where = jnp.stack([me, me % 2, group % 2]).astype(jnp.int32)
    hidden, a_in, a_out = hidden_slots[0], adapter_in[0], adapter_out[0]
    width = a_out.shape[1]
    half = width // 2
    wide = half // CHUNKS
    tokens = cotangent.shape[0]
    capacity = hidden.shape[0] // experts
    struct = jax.ShapeDtypeStruct

    def swap(x, bit):
        return lax.ppermute(x, "expert", [(i, i ^ bit) for i in range(experts)])

    def swap_side(x):
        return lax.ppermute(x, "group", [(i, i ^ 1) for i in range(groups)])

    def spread(x):
        return lax.all_to_all(x, "expert", split_axis=0, concat_axis=0, tiled=True)

    far_bits = []
    bit = 4
    while bit < experts:
        far_bits.append(bit)
        bit *= 2

    (block,) = call(
        half_factor_kernel,
        [struct((RANK, half), BF)],
        [a_out],
        where,
        scratch=[pltpu.SemaphoreType.DMA],
        spaces=[pl.ANY],
    )
    received = swap(block, 2)
    packed, own_meta = call(
        pack_tokens_kernel,
        [struct((tokens + 16, half), BF), struct((16, tokens), BF)],
        [cotangent, expert_ids.T, gate_weights.T],
        where,
        scratch=[pltpu.SemaphoreType.DMA],
        spaces=[pl.ANY, pltpu.VMEM, pltpu.VMEM],
    )
    packed = swap(packed, 1)
    low, stats = call(
        low_rank_kernel,
        [struct((RANK, hidden.shape[0]), BF), struct((RANK, 2 * capacity), BF)],
        [hidden, a_in, a_out],
        scratch=[pltpu.VMEM(hidden.shape, BF), pltpu.SemaphoreType.DMA],
        spaces=[pl.ANY, pltpu.VMEM, pltpu.VMEM],
    )
    (block,) = call(
        join_kernel, [struct((2 * RANK, half), BF)], [block, received], after=[own_meta, low]
    )
    (lows,) = call(
        pack_low_kernel,
        [struct((experts, RANK, 4 * capacity), BF)],
        [low, stats],
        after=[block],
    )
    lows = spread(lows)
    inv_in, inv_out = call(
        inverse_kernel, [struct((RANK, RANK), F32)] * 2, [a_in, a_out, lows]
    )
    count = experts * RANK // 2
    full = relative_order(far_bits)
    z, weights, *parts = call(
        lambda *refs: partial_kernel(full, *refs),
        [struct((tokens, experts * RANK), BF), struct((experts * capacity, tokens), BF)]
        + [struct((count, wide), F32)] * CHUNKS
        + [struct((count, wide), BF)] * CHUNKS,
        [cotangent, packed, own_meta, lows],
        where,
    )
    kept, sent = parts[:CHUNKS], parts[CHUNKS:]
    for bit in reversed(far_bits):
        received = swap(block, bit)
        if bit == far_bits[0]:
            near = [block, received]
        else:
            shape = (2 * block.shape[0], half)
            (block,) = call(
                join_kernel, [struct(shape, BF)], [block, received], after=[sent[0]]
            )
    own_rows, far_rows = [], []
    for piece in range(CHUNKS):
        keep, send, rows = kept[piece], sent[piece], count
        for bit in [2, *far_bits]:
            received = swap(send, bit)
            if bit == far_bits[-1]:
                shapes, step = [struct((RANK, wide), F32)] * 2, last_fold_kernel
            else:
                rows //= 2
                shapes = [struct((rows, wide), F32), struct((rows, wide), BF)]
                step = fold_step_kernel
            keep, send = call(step, shapes, [keep, received])
        own_rows.append(keep)
        far_rows.append(swap(send, 1))

    factors = []
    for block in near:
        factors += [block, swap_side(block)]
    factors = factors + [swap(block, 1) for block in factors]
    coords, delta = call(
        lambda *refs: factor_kernel(full, *refs),
        [struct((experts, RANK, 4 * capacity), BF), struct((tokens, width), BF)],
        [cotangent, weights, z, *factors],
        where,
        scratch=[
            pltpu.VMEM(cotangent.shape, BF),
            pltpu.VMEM((2, experts * RANK, half), BF),
            pltpu.SemaphoreType.DMA((9,)),
        ],
        spaces=[pl.ANY, pltpu.VMEM, pltpu.VMEM] + [pl.ANY] * 8,
    )
    coords = spread(coords)
    (scaled_in,) = call(
        scaled_in_kernel, [struct((RANK, hidden.shape[1]), F32)], [coords, hidden, inv_out]
    )
    (scaled_out,) = call(
        scaled_out_kernel, [struct((RANK, width), F32)], [inv_in, *own_rows, *far_rows], where
    )
    return delta, scaled_in[None], scaled_out[None]


def solution(mesh):
    every = ("group", "expert")
    return jax.shard_map(
        on_device,
        mesh=mesh,
        in_specs=(
            P(every, None, None),
            P("expert", None, None),
            P("expert", None, None),
            P(every, None),
            P(every, None),
            P(every, None),
        ),
        out_specs=(P(every, None), P(every, None, None), P(every, None, None)),
        check_vma=False,
    )
```

```python
import jax
import jax.numpy as jnp
import numpy as np
from jax import lax
from jax.experimental import pallas as pl
from jax.experimental.pallas import tpu as pltpu
from jax.sharding import PartitionSpec as P

BF = jnp.bfloat16
F32 = jnp.float32
HIGHEST = lax.Precision.HIGHEST
RANK = 16
CHUNKS = 2
HBM = pltpu.HBM
VMEM = pltpu.VMEM
DMA = pltpu.SemaphoreType.DMA
MIB = 1024 * 1024


def mm(a, b, ca=1, cb=0, precision=None):
    return lax.dot_general(
        a, b, (((ca,), (cb,)), ((), ())), preferred_element_type=F32, precision=precision
    )


def call(
    kernel, outs, args, scalars=None, after=(), scratch=(), spaces=None, out_spaces=None, alias=None, limit=None
):
    size = sum(x.size * x.dtype.itemsize for x in [*args, *outs])
    total = size + sum(
        np.prod(x.shape) * x.dtype.itemsize for x in scratch if len(getattr(x, "shape", ())) > 1
    )
    specs = [pl.BlockSpec(memory_space=space) for space in spaces or [VMEM] * len(args)]
    out_spaces = out_spaces or [VMEM] * len(outs)
    if scalars is not None:
        args = [scalars, *args]
        specs = [pl.BlockSpec(memory_space=pltpu.SMEM), *specs]
    used = len(args)

    def body(*refs):
        kernel(*refs[:used], *refs[used + len(after) :])

    return pl.pallas_call(
        body,
        out_shape=[jax.ShapeDtypeStruct(o.shape, o.dtype) for o in outs],
        in_specs=specs + [pl.BlockSpec(memory_space=pl.ANY)] * len(after),
        out_specs=[pl.BlockSpec(memory_space=space) for space in out_spaces],
        scratch_shapes=list(scratch),
        input_output_aliases=alias or {},
        compiler_params=pltpu.CompilerParams(
            vmem_limit_bytes=limit or min(60 * MIB, int(8 * MIB + 1.5 * total))
        ),
        cost_estimate=pl.CostEstimate(flops=0, bytes_accessed=size, transcendentals=0),
    )(*args, *after)


def split(x):
    high = x.astype(BF)
    return high, (x - high.astype(F32)).astype(BF)


def lanes(start, size):
    return pl.ds(pl.multiple_of(start, 128), size)


def low_rank_kernel(hidden, a_in, a_out, low_out, stats_out, hidden_in, a_in_in, a_out_in, sems):
    slots = stats_out.shape[1]
    pieces = 4
    rows = hidden.shape[0] // pieces
    copies = [
        pltpu.make_async_copy(a_in, a_in_in, sems.at[pieces]),
        pltpu.make_async_copy(a_out, a_out_in, sems.at[pieces + 1]),
    ]
    for i in range(pieces):
        part = pl.ds(i * rows, rows)
        copies.append(pltpu.make_async_copy(hidden.at[part], hidden_in.at[part], sems.at[i]))
    for copy in copies:
        copy.start()
    copies[0].wait()
    copies[1].wait()
    row = lax.broadcasted_iota(jnp.int32, (RANK, slots), 0)
    stats = jnp.zeros((RANK, slots), F32)
    for base, factor in ((0, a_in_in), (3, a_out_in)):
        square = jnp.square(factor[...].astype(F32))
        rest = jnp.sum(jnp.sum(square, axis=1, keepdims=True), axis=0, keepdims=True)
        rest = jnp.broadcast_to(rest, (RANK, slots))
        for piece in range(3):
            part = rest.astype(BF).astype(F32)
            stats = jnp.where(row == base + piece, part, stats)
            rest = rest - part
    stats_out[...] = stats.astype(BF)
    for i in range(pieces):
        copies[2 + i].wait()
        part = slice(i * rows, (i + 1) * rows)
        low_out[:, part] = mm(a_in_in[...], hidden_in[part, :], 1, 1).astype(BF)


def pack_low_kernel(low, stats, out):
    slots = out.shape[2] // 2
    for device in range(out.shape[0]):
        chip = device // 2
        out[device, :, 0:slots] = low[:, chip * slots : (chip + 1) * slots]
        out[device, :, slots:] = stats[...]


def join_kernel(*refs):
    pieces, out = refs[:-1], refs[-1]
    start = 0
    for piece in pieces:
        out[start : start + piece.shape[0], :] = piece[...]
        start += piece.shape[0]


def fold_of(slots, experts, capacity, source):
    column = lax.broadcasted_iota(jnp.int32, (slots, experts * capacity), 1)
    row = lax.broadcasted_iota(jnp.int32, (slots, experts * capacity), 0)
    return (row == source * capacity + lax.rem(column, capacity)).astype(BF)


def own_expert(experts, capacity):
    shape = (experts * RANK, experts * capacity)
    row = lax.div(lax.broadcasted_iota(jnp.int32, shape, 0), RANK)
    column = lax.div(lax.broadcasted_iota(jnp.int32, shape, 1), capacity)
    return row == column


def relative_experts(order_size, tokens, me):
    row = lax.broadcasted_iota(jnp.int32, (order_size, tokens), 0)
    return jnp.bitwise_xor(row, me).astype(F32)


def partial_kernel(order, where, cot, packed, own_meta, far_meta, lows, z_out, w_out, *outs):
    keeps, sends = outs[:CHUNKS], outs[CHUNKS : 2 * CHUNKS]
    own_in, sem = outs[2 * CHUNKS :]
    me, core = where[0], where[1]
    experts, tokens = lows.shape[0], cot.shape[0]
    slots = lows.shape[2] // 2
    capacity = slots // 2
    half = packed.shape[1]
    copy = pltpu.make_async_copy(cot.at[:, lanes(core * half, half)], own_in, sem)
    copy.start()
    low = jnp.concatenate(
        [lows[jnp.bitwise_xor(me, e)][:, 0:slots] for e in range(experts)], axis=0
    )
    own = own_expert(experts, capacity)
    expert = relative_experts(experts, tokens, me)
    earlier = (
        lax.broadcasted_iota(jnp.int32, (tokens, tokens), 0)
        < lax.broadcasted_iota(jnp.int32, (tokens, tokens), 1)
    ).astype(BF)
    place = lax.broadcasted_iota(jnp.int32, (experts, capacity, tokens), 1).astype(F32)
    rows = []
    for s in range(2):
        meta = (own_meta if s == 0 else far_meta)[...].astype(F32)
        first = (meta[0:1] == expert).astype(F32)
        second = (meta[1:2] == expert).astype(F32)
        before = mm((first + second).astype(BF), earlier)
        gate = first * meta[2:3] + second * meta[3:4]
        spread = jnp.where(before[:, None, :] == place, gate[:, None, :], 0.0)
        weights = spread.reshape(experts * capacity, tokens).astype(BF)
        source = jnp.bitwise_xor(core, s)
        wide = mm(low, fold_of(slots, experts, capacity, source))
        wide = jnp.where(own, wide, 0.0).astype(BF)
        exact = mm(wide, weights)
        z = exact.astype(BF)
        rows.append(z.reshape(experts // 4, 2, 2 * RANK, tokens))
        if s == 0:
            w_out[...] = weights
            ordered = jnp.concatenate([exact[e * RANK : (e + 1) * RANK] for e in order], axis=0)
            z_out[...] = ordered.T.astype(BF)
    count = experts * RANK // 2
    copy.wait()
    base = 0
    for keep, send in zip(keeps, sends):
        here = slice(base, base + keep.shape[1])
        base += keep.shape[1]
        for side, target in ((0, keep), (1, send)):
            first = rows[0][:, side].reshape(count, tokens)
            second = rows[1][:, side].reshape(count, tokens)
            total = mm(first, own_in[:, here]) + mm(second, packed[:, here])
            target[...] = total.astype(target.dtype)


def fold_step_kernel(received, keep, *refs):
    sends, kept = refs[received:-1], refs[-1]
    rows, width = keep.shape
    radix = 1 + len(sends)
    total = keep[...]
    for more in refs[:received]:
        total = total + more[...].astype(F32)
    total = total.reshape(rows // (2 * RANK * radix), radix, 2 * RANK, width)
    kept[...] = total[:, 0].reshape(kept.shape)
    for i, send in enumerate(sends):
        send[...] = total[:, i + 1].reshape(send.shape).astype(send.dtype)


def last_fold_kernel(keep, *refs):
    received, (kept, sent) = refs[:-2], refs[-2:]
    total = keep[...]
    for more in received:
        total = total + more[...].astype(F32)
    kept[...] = total[0:RANK]
    sent[...] = total[RANK:]


def factor_half(flip, side, cot, z, factors, delta, scratch):
    tokens_in, table, result, sems = scratch
    tokens, half = tokens_in.shape
    lane = lanes(jnp.bitwise_xor(side, flip) * half, half)
    copies = [pltpu.make_async_copy(cot.at[:, lane], tokens_in, sems.at[len(factors)])]
    start = 0
    for i, factor in enumerate(factors):
        size = factor.shape[0]
        target = table.at[start : start + size, :]
        copies.append(pltpu.make_async_copy(factor, target, sems.at[i]))
        start += size
    for copy in copies:
        copy.start()
    for copy in copies:
        copy.wait()
    cut = half // 4
    coords = jnp.zeros((start, tokens), F32)
    copies = []
    for piece in range(4):
        here = slice(piece * cut, (piece + 1) * cut)
        result[:, here] = mm(z[...], table[:, here]).astype(BF)
        target = delta.at[:, lanes(jnp.bitwise_xor(side, flip) * half + piece * cut, cut)]
        copies.append(pltpu.make_async_copy(result.at[:, here], target, sems.at[piece]))
        copies[-1].start()
        coords = coords + mm(table[:, here], tokens_in[:, here], 1, 1)
    return coords, copies


def near_kernel(where, cot, z, *refs):
    factors, (coords_out, delta), scratch = refs[:-6], refs[-6:-4], refs[-4:]
    coords_out[...], copies = factor_half(0, where[2], cot, z, factors, delta, scratch)
    for copy in copies:
        copy.wait()


def far_kernel(order, where, cot, z, w, near, _, *refs):
    factors, (coords_out, delta), scratch = refs[:-6], refs[-6:-4], refs[-4:]
    experts, _, slots = coords_out.shape
    capacity = slots // 4
    coords, copies = factor_half(1, where[2], cot, z, factors, delta, scratch)
    coords = coords + near[...]
    blocks = [order.index(e) * RANK for e in range(experts)]
    coords = jnp.concatenate([coords[b : b + RANK] for b in blocks], axis=0)
    high, low = split(coords)
    picked = mm(high, w[...], 1, 1) + mm(low, w[...], 1, 1)
    picked = jnp.where(own_expert(experts, capacity), picked, 0.0).astype(BF)
    fold = fold_of(slots, experts, capacity, lax.rem(where[0], 4))
    rows = mm(picked, fold, 1, 1).astype(coords_out.dtype)
    for e in range(experts):
        coords_out[jnp.bitwise_xor(where[0], e)] = rows[e * RANK : (e + 1) * RANK]
    for copy in copies:
        copy.wait()


def inverse_kernel(a_in, a_out, lows, inv_in, inv_out):
    experts, _, double = lows.shape
    stats = jnp.sum(lows[:, :, double // 2 :].astype(F32), axis=0)
    row = lax.broadcasted_iota(jnp.int32, (RANK, RANK), 0)
    column = lax.broadcasted_iota(jnp.int32, (RANK, RANK), 1)
    eye = (row == column).astype(F32)
    works = []
    for base, factor in ((0, a_in), (3, a_out)):
        pieces = stats[base : base + 1, 0:1] + stats[base + 1 : base + 2, 0:1]
        damp = (pieces + stats[base + 2 : base + 3, 0:1]) / (float(RANK) * experts)
        gram = mm(factor[...], factor[...], 1, 1) + damp * eye
        works.append([gram, eye])
    for j in range(RANK):
        for work in works:
            gram, inverse = work
            pivot = 1.0 / gram[j : j + 1, j : j + 1]
            gram_row, inverse_row = gram[j : j + 1] * pivot, inverse[j : j + 1] * pivot
            scale = gram[:, j : j + 1]
            work[0] = jnp.where(row == j, gram_row, gram - scale * gram_row)
            work[1] = jnp.where(row == j, inverse_row, inverse - scale * inverse_row)
    inv_in[...] = works[0][1]
    inv_out[...] = works[1][1]


def scaled_in_kernel(coords, hidden, inverse, out):
    pieces = []
    for base in range(0, coords.shape[0], 4):
        total = coords[base].astype(F32)
        for q in range(1, 4):
            total = total + coords[base + q].astype(F32)
        pieces.append(total)
    grad_low = jnp.concatenate(pieces, axis=1).astype(BF)
    out[...] = mm(inverse[...], mm(grad_low, hidden[...]), precision=HIGHEST)


def scaled_out_kernel(where, inverse, *refs):
    pieces, out = refs[:-1], refs[-1]
    half = out.shape[1] // 2
    for flip in range(2):
        base = jnp.bitwise_xor(where[1], flip) * half
        for piece in pieces[flip * CHUNKS : (flip + 1) * CHUNKS]:
            rows = mm(inverse[...], piece[...], precision=HIGHEST)
            out[:, lanes(base, piece.shape[1])] = rows
            base = base + piece.shape[1]


def radix_groups(experts):
    groups, bit = [], 4
    while bit < experts:
        radix = min(4, experts // bit)
        groups.append([bit * k for k in range(1, radix)])
        bit *= radix
    return groups


def relative_order(bits):
    order = [0]
    for bit in bits:
        order = order + [e ^ bit for e in order]
    return order


def on_device(hidden_slots, adapter_in, adapter_out, expert_ids, gate_weights, cotangent):
    experts, groups = lax.axis_size("expert"), lax.axis_size("group")
    me, group = lax.axis_index("expert"), lax.axis_index("group")
    where = jnp.stack([me, me % 2, group % 2]).astype(jnp.int32)
    hidden, a_in, a_out = hidden_slots[0], adapter_in[0], adapter_out[0]
    width = a_out.shape[1]
    half = width // 2
    tokens = cotangent.shape[0]
    capacity = hidden.shape[0] // experts
    struct = jax.ShapeDtypeStruct

    def swap(x, bit):
        return lax.ppermute(x, "expert", [(i, i ^ bit) for i in range(experts)])

    def swap_side(x):
        return lax.ppermute(x, "group", [(i, i ^ 1) for i in range(groups)])

    def spread(x):
        return lax.all_to_all(x, "expert", split_axis=0, concat_axis=0, tiled=True)

    groups_z = radix_groups(experts)
    far_bits = [1 << i for i in reversed(range(2, experts.bit_length() - 1))]
    full = relative_order([2, *far_bits, 1])

    block = lax.dynamic_slice_in_dim(a_out, (group % 2) * half, half, axis=1)
    received = swap(block, 2)
    low, stats = call(
        low_rank_kernel,
        [struct((RANK, hidden.shape[0]), BF), struct((RANK, 2 * capacity), BF)],
        [hidden, a_in, a_out],
        scratch=[
            VMEM(hidden.shape, BF),
            VMEM(a_in.shape, BF),
            VMEM(a_out.shape, BF),
            DMA((6,)),
        ],
        spaces=[HBM] * 3,
        limit=63 * MIB,
    )
    far_tokens = lax.dynamic_slice_in_dim(cotangent, (1 - me % 2) * half, half, axis=1)
    far_tokens = swap(far_tokens, 1)
    own_meta = jnp.concatenate(
        [expert_ids.T.astype(BF), gate_weights.T.astype(BF), jnp.zeros((12, tokens), BF)], axis=0
    )
    far_meta = swap(own_meta, 1)
    (block,) = call(
        join_kernel, [struct((2 * RANK, half), BF)], [block, received], after=[low]
    )
    (lows,) = call(
        pack_low_kernel,
        [struct((experts, RANK, 4 * capacity), BF)],
        [low, stats],
        after=[block],
    )
    lows = spread(lows)
    inv_in, inv_out = call(
        inverse_kernel, [struct((RANK, RANK), F32)] * 2, [a_in, a_out, lows]
    )
    count = experts * RANK // 2
    for bit in far_bits:
        received = swap(block, bit)
        if bit == far_bits[-1]:
            near = [block, received]
        else:
            (block,) = call(
                join_kernel,
                [struct((2 * block.shape[0], half), BF)],
                [block, received],
                after=[lows],
            )
    tiles = half // 128
    wides = [128 * (tiles // 2), half - 128 * (tiles // 2)]
    z, weights, *parts = call(
        lambda *refs: partial_kernel(full, *refs),
        [struct((tokens, experts * RANK), BF), struct((experts * capacity, tokens), BF)]
        + [struct((count, wide), F32) for wide in wides]
        + [struct((count, wide), BF) for wide in wides],
        [cotangent, far_tokens, own_meta, far_meta, lows],
        where,
        after=[near[0]],
        scratch=[VMEM((tokens, half), BF), DMA],
        spaces=[HBM, VMEM, VMEM, VMEM, VMEM],
    )
    kept, sent = parts[:CHUNKS], parts[CHUNKS:]
    near[1:] = call(
        join_kernel, [struct(near[1].shape, BF)], [near[1]], after=[sent[0]]
    )
    factors, far = list(near), [swap_side(block) for block in near]

    factors += [swap(block, 1) for block in near]
    far += [swap(block, 1) for block in far]
    scratch = [
        VMEM((tokens, half), BF),
        VMEM((experts * RANK, half), BF),
        VMEM((tokens, half), BF),
        DMA((2 * len(near) + 1,)),
    ]
    near_coords, delta = call(
        near_kernel,
        [struct((experts * RANK, tokens), F32), struct((tokens, width), BF)],
        [cotangent, z, *factors],
        where,
        scratch=scratch,
        spaces=[HBM, VMEM] + [HBM] * len(factors),
        out_spaces=[VMEM, HBM],
    )
    coords, delta = call(
        lambda *refs: far_kernel(full, *refs),
        [struct((experts, RANK, 4 * capacity), BF), struct((tokens, width), BF)],
        [cotangent, z, weights, near_coords, delta, *far],
        where,
        scratch=scratch,
        spaces=[HBM, VMEM, VMEM, VMEM, HBM] + [HBM] * len(far),
        out_spaces=[VMEM, HBM],
        alias={5: 1},
    )
    own_rows, far_rows = [], []
    for piece in range(CHUNKS):
        keep, rows, wide = kept[piece], count, wides[piece]
        received = [swap(sent[piece], 2)]
        for group in groups_z:
            radix = 1 + len(group)
            rows //= radix
            if piece == 0:
                total = keep
                for more in received:
                    total = total + more.astype(F32)
                total = total.reshape(rows // (2 * RANK), radix, 2 * RANK, wide)
                keep = total[:, 0].reshape(rows, wide)
                sends = [total[:, k].reshape(rows, wide).astype(BF) for k in range(1, radix)]
            else:
                *sends, keep = call(
                    lambda keep, *refs, n=len(received): fold_step_kernel(n, keep, *refs),
                    [struct((rows, wide), BF)] * len(group) + [struct((rows, wide), F32)],
                    [keep, *received],
                    after=[near_coords, far[1]],
                )
            received = [swap(send, k) for send, k in zip(sends, group)]
        if piece == 0:
            for more in received:
                keep = keep + more.astype(F32)
            keep, send = keep[:RANK], keep[RANK:]
        else:
            keep, send = call(
                last_fold_kernel,
                [struct((RANK, wide), F32)] * 2,
                [keep, *received],
                after=[coords],
            )
        own_rows.append(keep)
        far_rows.append(swap(send, 1))

    coords = spread(coords)
    (scaled_in,) = call(
        scaled_in_kernel, [struct((RANK, hidden.shape[1]), F32)], [coords, hidden, inv_out]
    )
    (scaled_out,) = call(
        scaled_out_kernel, [struct((RANK, width), F32)], [inv_in, *own_rows, *far_rows], where
    )
    return delta, scaled_in[None], scaled_out[None]


def solution(mesh):
    every = ("group", "expert")
    return jax.shard_map(
        on_device,
        mesh=mesh,
        in_specs=(
            P(every, None, None),
            P("expert", None, None),
            P("expert", None, None),
            P(every, None),
            P(every, None),
            P(every, None),
        ),
        out_specs=(P(every, None), P(every, None, None), P(every, None, None)),
        check_vma=False,
    )
```

```python
import jax
import jax.numpy as jnp
import numpy as np
from jax import lax
from jax.experimental import pallas as pl
from jax.experimental.pallas import tpu as pltpu
from jax.sharding import PartitionSpec as P
BF = jnp.bfloat16
F32 = jnp.float32
HIGHEST = lax.Precision.HIGHEST
RANK = 16
CHUNKS = 2
HBM = pltpu.HBM
VMEM = pltpu.VMEM
DMA = pltpu.SemaphoreType.DMA
MIB = 1024 * 1024


def mm(a, b, ca=1, cb=0, precision=None):
    return lax.dot_general(a, b, (((ca,), (cb,)), ((), ())), preferred_element_type=F32, precision=precision)


def call(kernel, outs, args, scalars=None, after=(), scratch=(), spaces=None, out_spaces=None, alias=None, limit=None):
    size = sum((x.size * x.dtype.itemsize for x in [*args, *outs]))
    total = size + sum((np.prod(x.shape) * x.dtype.itemsize for x in scratch if hasattr(x.dtype, 'itemsize')))
    specs = [pl.BlockSpec(memory_space=space) for space in spaces or [VMEM] * len(args)]
    out_spaces = out_spaces or [VMEM] * len(outs)
    if scalars is not None:
        args = [scalars, *args]
        specs = [pl.BlockSpec(memory_space=pltpu.SMEM), *specs]
    used = len(args)

    def body(*refs):
        kernel(*refs[:used], *refs[used + len(after):])
    return pl.pallas_call(body, out_shape=[jax.ShapeDtypeStruct(o.shape, o.dtype) for o in outs], in_specs=specs + [pl.BlockSpec(memory_space=pl.ANY)] * len(after), out_specs=[pl.BlockSpec(memory_space=space) for space in out_spaces], scratch_shapes=list(scratch), input_output_aliases=alias or {}, compiler_params=pltpu.CompilerParams(vmem_limit_bytes=limit or min(60 * MIB, int(8 * MIB + 1.5 * total))), cost_estimate=pl.CostEstimate(flops=0, bytes_accessed=size, transcendentals=0))(*args, *after)


def split(x):
    high = x.astype(BF)
    return (high, (x - high.astype(F32)).astype(BF))


def lanes(start, size):
    return pl.ds(pl.multiple_of(start, 128), size)


def low_rank_kernel(hidden, a_in, a_out, low_out, stats_out, hidden_in, a_in_in, a_out_in, sems):
    slots = stats_out.shape[1]
    pieces = 4
    rows = hidden.shape[0] // pieces
    copies = [pltpu.make_async_copy(a_in, a_in_in, sems.at[pieces]), pltpu.make_async_copy(a_out, a_out_in, sems.at[pieces + 1])]
    for i in range(pieces):
        part = pl.ds(i * rows, rows)
        copies.append(pltpu.make_async_copy(hidden.at[part], hidden_in.at[part], sems.at[i]))
    for copy in copies:
        copy.start()
    copies[0].wait()
    copies[1].wait()
    row = lax.broadcasted_iota(jnp.int32, (RANK, slots), 0)
    stats = jnp.zeros((RANK, slots), F32)
    for base, factor in ((0, a_in_in), (3, a_out_in)):
        square = jnp.square(factor[...].astype(F32))
        rest = jnp.sum(jnp.sum(square, axis=1, keepdims=True), axis=0, keepdims=True)
        rest = jnp.broadcast_to(rest, (RANK, slots))
        for piece in range(3):
            part = rest.astype(BF).astype(F32)
            stats = jnp.where(row == base + piece, part, stats)
            rest = rest - part
    stats_out[...] = stats.astype(BF)
    for i in range(pieces):
        copies[2 + i].wait()
        part = slice(i * rows, (i + 1) * rows)
        low_out[:, part] = mm(a_in_in[...], hidden_in[part, :], 1, 1).astype(BF)


def pack_low_kernel(low, stats, out):
    slots = out.shape[2] // 2
    for device in range(out.shape[0]):
        chip = device // 2
        out[device, :, 0:slots] = low[:, chip * slots:(chip + 1) * slots]
        out[device, :, slots:] = stats[...]


def join_kernel(*refs):
    pieces, out = (refs[:-1], refs[-1])
    start = 0
    for piece in pieces:
        out[start:start + piece.shape[0], :] = piece[...]
        start += piece.shape[0]


def fold_of(slots, experts, capacity, source):
    column = lax.broadcasted_iota(jnp.int32, (slots, experts * capacity), 1)
    row = lax.broadcasted_iota(jnp.int32, (slots, experts * capacity), 0)
    return (row == source * capacity + lax.rem(column, capacity)).astype(BF)


def own_expert(experts, capacity):
    shape = (experts * RANK, experts * capacity)
    row = lax.div(lax.broadcasted_iota(jnp.int32, shape, 0), RANK)
    column = lax.div(lax.broadcasted_iota(jnp.int32, shape, 1), capacity)
    return row == column


def relative_experts(order_size, tokens, me):
    row = lax.broadcasted_iota(jnp.int32, (order_size, tokens), 0)
    return jnp.bitwise_xor(row, me).astype(F32)


def weights_of(where, order, own_meta, far_meta, lows, z_out, w_out):
    me, core = (where[0], where[1])
    experts, tokens = (lows.shape[0], own_meta.shape[1])
    slots = lows.shape[2] // 2
    capacity = slots // 2
    low = jnp.concatenate([lows[jnp.bitwise_xor(me, e)][:, 0:slots] for e in range(experts)], axis=0)
    own = own_expert(experts, capacity)
    expert = relative_experts(experts, tokens, me)
    earlier = (lax.broadcasted_iota(jnp.int32, (tokens, tokens), 0) < lax.broadcasted_iota(jnp.int32, (tokens, tokens), 1)).astype(BF)
    place = lax.broadcasted_iota(jnp.int32, (experts, capacity, tokens), 1).astype(F32)
    rows = []
    for s in range(2):
        meta = (own_meta if s == 0 else far_meta)[...].astype(F32)
        first = (meta[0:1] == expert).astype(F32)
        second = (meta[1:2] == expert).astype(F32)
        before = mm((first + second).astype(BF), earlier)
        gate = first * meta[2:3] + second * meta[3:4]
        spread = jnp.where(before[:, None, :] == place, gate[:, None, :], 0.0)
        weights = spread.reshape(experts * capacity, tokens).astype(BF)
        source = jnp.bitwise_xor(core, s)
        wide = mm(low, fold_of(slots, experts, capacity, source))
        wide = jnp.where(own, wide, 0.0).astype(BF)
        exact = mm(wide, weights)
        rows.append(exact.astype(BF))
        if s == 0:
            w_out[...] = weights
            ordered = jnp.concatenate([exact[e * RANK:(e + 1) * RANK] for e in order], axis=0)
            z_out[...] = ordered.T.astype(BF)
    return rows


def product_of(rows, own_in, far_in, here, keep, send):
    count, tokens = (keep.shape[0], rows[0].shape[1])
    groups = rows[0].shape[0] // (4 * RANK)
    for side, target in ((0, keep), (1, send)):
        first, second = (r.reshape(groups, 2, 2 * RANK, tokens)[:, side].reshape(count, tokens) for r in rows)
        total = mm(first, own_in[:, here]) + mm(second, far_in[:, here])
        target[...] = total.astype(target.dtype)


def token_copies(where, cot, packed, own_in, far_in, sems):
    half = own_in.shape[1]
    here = lanes(where[1] * half, half)
    copies = [pltpu.make_async_copy(cot.at[:, here], own_in, sems.at[0])]
    source = packed if packed.shape[1] == half else packed.at[:, here]
    copies.append(pltpu.make_async_copy(source, far_in, sems.at[1]))
    for copy in copies:
        copy.start()
    return copies


def partial_kernel(order, where, cot, packed, own_meta, far_meta, lows, z_out, w_out, *outs):
    keeps, sends = (outs[:CHUNKS], outs[CHUNKS:2 * CHUNKS])
    own_in, far_in, sems = outs[2 * CHUNKS:]
    copies = token_copies(where, cot, packed, own_in, far_in, sems)
    rows = weights_of(where, order, own_meta, far_meta, lows, z_out, w_out)
    for copy in copies:
        copy.wait()
    base = 0
    for keep, send in zip(keeps, sends):
        here = slice(base, base + keep.shape[1])
        base += keep.shape[1]
        product_of(rows, own_in, far_in, here, keep, send)


def fold_step_kernel(received, keep, *refs):
    sends, kept = (refs[received:-1], refs[-1])
    rows, width = keep.shape
    radix = 1 + len(sends)
    total = keep[...]
    for more in refs[:received]:
        total = total + more[...].astype(F32)
    total = total.reshape(rows // (2 * RANK * radix), radix, 2 * RANK, width)
    kept[...] = total[:, 0].reshape(kept.shape)
    for i, send in enumerate(sends):
        send[...] = total[:, i + 1].reshape(send.shape).astype(send.dtype)


def last_fold_kernel(keep, *refs):
    received, (kept, sent) = (refs[:-2], refs[-2:])
    total = keep[...]
    for more in received:
        total = total + more[...].astype(F32)
    kept[...] = total[0:RANK]
    sent[...] = total[RANK:]


def factor_half(flip, side, cot, z, factors, delta, scratch):
    tokens_in, table, result, sems = scratch
    pieces, tokens, cut = tokens_in.shape
    base = jnp.bitwise_xor(side, flip) * (pieces * cut)
    copies = []
    for piece in range(pieces):
        moves = [(cot.at[:, lanes(base + piece * cut, cut)], tokens_in.at[piece])]
        start = 0
        for factor in factors:
            size = factor.shape[0]
            source = factor.at[:, piece * cut:(piece + 1) * cut]
            moves.append((source, table.at[piece, start:start + size, :]))
            start += size
        copies.append([pltpu.make_async_copy(source, target, sems.at[piece, i]) for i, (source, target) in enumerate(moves)])
        for copy in copies[-1]:
            copy.start()
    coords = jnp.zeros((start, tokens), F32)
    writes = []
    for piece in range(pieces):
        for copy in copies[piece]:
            copy.wait()
        block = table[piece]
        result[piece] = mm(z[...], block).astype(BF)
        target = delta.at[:, lanes(base + piece * cut, cut)]
        writes.append(pltpu.make_async_copy(result.at[piece], target, sems.at[piece, len(factors) + 1]))
        writes[-1].start()
        coords = coords + mm(block, tokens_in[piece], 1, 1)
    return (coords, writes)


def near_kernel(where, cot, z, *refs):
    factors, (coords_out, delta), scratch = (refs[:-6], refs[-6:-4], refs[-4:])
    coords_out[...], copies = factor_half(0, where[2], cot, z, factors, delta, scratch)
    for copy in copies:
        copy.wait()


def far_kernel(order, where, cot, z, w, near, _, *refs):
    factors, (coords_out, delta), scratch = (refs[:-6], refs[-6:-4], refs[-4:])
    experts, _, slots = coords_out.shape
    capacity = slots // 4
    coords, copies = factor_half(1, where[2], cot, z, factors, delta, scratch)
    coords = coords + near[...]
    blocks = [order.index(e) * RANK for e in range(experts)]
    coords = jnp.concatenate([coords[b:b + RANK] for b in blocks], axis=0)
    high, low = split(coords)
    picked = mm(high, w[...], 1, 1) + mm(low, w[...], 1, 1)
    picked = jnp.where(own_expert(experts, capacity), picked, 0.0).astype(BF)
    fold = fold_of(slots, experts, capacity, lax.rem(where[0], 4))
    rows = mm(picked, fold, 1, 1).astype(coords_out.dtype)
    for e in range(experts):
        coords_out[jnp.bitwise_xor(where[0], e)] = rows[e * RANK:(e + 1) * RANK]
    for copy in copies:
        copy.wait()


def inverse_kernel(a_in, a_out, lows, inv_in, inv_out):
    experts, _, double = lows.shape
    stats = jnp.sum(lows[:, :, double // 2:].astype(F32), axis=0)
    row = lax.broadcasted_iota(jnp.int32, (RANK, RANK), 0)
    column = lax.broadcasted_iota(jnp.int32, (RANK, RANK), 1)
    eye = (row == column).astype(F32)
    works = []
    for base, factor in ((0, a_in), (3, a_out)):
        pieces = stats[base:base + 1, 0:1] + stats[base + 1:base + 2, 0:1]
        damp = (pieces + stats[base + 2:base + 3, 0:1]) / (float(RANK) * experts)
        gram = mm(factor[...], factor[...], 1, 1) + damp * eye
        works.append([gram, eye])
    for j in range(RANK):
        for work in works:
            gram, inverse = work
            pivot = 1.0 / gram[j:j + 1, j:j + 1]
            gram_row, inverse_row = (gram[j:j + 1] * pivot, inverse[j:j + 1] * pivot)
            scale = gram[:, j:j + 1]
            work[0] = jnp.where(row == j, gram_row, gram - scale * gram_row)
            work[1] = jnp.where(row == j, inverse_row, inverse - scale * inverse_row)
    inv_in[...] = works[0][1]
    inv_out[...] = works[1][1]


def scaled_in_kernel(coords, hidden, inverse, out):
    pieces = []
    for base in range(0, coords.shape[0], 4):
        total = coords[base].astype(F32)
        for q in range(1, 4):
            total = total + coords[base + q].astype(F32)
        pieces.append(total)
    grad_low = jnp.concatenate(pieces, axis=1).astype(BF)
    out[...] = mm(inverse[...], mm(grad_low, hidden[...]), precision=HIGHEST)


def scaled_out_kernel(where, inverse, *refs):
    pieces, (out, rows, sems) = (refs[:-3], refs[-3:])
    half = out.shape[1] // 2
    copies, starts = ([], [0, 0])
    for i, piece in enumerate(pieces):
        flip, width = (i % 2, piece.shape[1])
        base = jnp.bitwise_xor(where[1], flip) * half + starts[flip]
        starts[flip] += width
        rows[i, :, 0:width] = mm(inverse[...], piece[...], precision=HIGHEST)
        target = out.at[:, lanes(base, width)]
        copies.append(pltpu.make_async_copy(rows.at[i, :, 0:width], target, sems.at[i]))
        copies[-1].start()
    for copy in copies:
        copy.wait()


def radix_groups(experts, most):
    groups, bit = ([], 4)
    while bit < experts:
        radix = min(most, experts // bit)
        groups.append([bit * k for k in range(1, radix)])
        bit *= radix
    return groups


def relative_order(bits):
    order = [0]
    for bit in bits:
        order = order + [e ^ bit for e in order]
    return order


def on_device(hidden_slots, adapter_in, adapter_out, expert_ids, gate_weights, cotangent):
    experts, groups = (lax.axis_size('expert'), lax.axis_size('group'))
    me, group = (lax.axis_index('expert'), lax.axis_index('group'))
    where = jnp.stack([me, me % 2, group % 2]).astype(jnp.int32)
    hidden, a_in, a_out = (hidden_slots[0], adapter_in[0], adapter_out[0])
    width = a_out.shape[1]
    half = width // 2
    tokens = cotangent.shape[0]
    capacity = hidden.shape[0] // experts
    struct = jax.ShapeDtypeStruct

    def swap(x, bit):
        return lax.ppermute(x, 'expert', [(i, i ^ bit) for i in range(experts)])

    def swap_side(x):
        return lax.ppermute(x, 'group', [(i, i ^ 1) for i in range(groups)])

    def spread(x):
        return lax.all_to_all(x, 'expert', split_axis=0, concat_axis=0, tiled=True)
    groups_z = radix_groups(experts, 4)
    groups_of = [radix_groups(experts, 2 if 0 & 1 << p else 4) for p in range(2)]
    far_bits = [1 << i for i in reversed(range(2, experts.bit_length() - 1))]
    full = relative_order([2, *far_bits, 1])
    block = jnp.where(group % 2 == 0, a_out[:, :half], a_out[:, half:])
    received = swap(block, 2)
    low, stats = call(low_rank_kernel, [struct((RANK, hidden.shape[0]), BF), struct((RANK, 2 * capacity), BF)], [hidden, a_in, a_out], scratch=[VMEM(hidden.shape, BF), VMEM(a_in.shape, BF), VMEM(a_out.shape, BF), DMA((6,))], spaces=[HBM] * 3, limit=63 * MIB)
    far_tokens = swap(cotangent, 1)
    own_meta = jnp.concatenate([expert_ids.T.astype(BF), gate_weights.T.astype(BF), jnp.zeros((12, tokens), BF)], axis=0)
    far_meta = swap(own_meta, 1)
    block, = call(join_kernel, [struct((2 * RANK, half), BF)], [block, received], after=[low])
    lows, = call(pack_low_kernel, [struct((experts, RANK, 4 * capacity), BF)], [low, stats], after=[block])
    lows = spread(lows)
    inv_in, inv_out = call(inverse_kernel, [struct((RANK, RANK), F32)] * 2, [a_in, a_out, lows])
    count = experts * RANK // 2

    def planes_of(block, gate):
        for bit in far_bits:
            received = swap(block, bit)
            if bit == far_bits[-1]:
                return ([block, received], last)
            last = [block, received]
            block, = call(join_kernel, [struct((2 * block.shape[0], half), BF)], last, after=gate)
    gate_inv = []
    early = []
    near, last = planes_of(block, [lows] + gate_inv)
    early = [near[0]]
    tiles = half // 128
    wides = [128 * (tiles * 14 // 28), half - 128 * (tiles * 14 // 28)]
    token_args = [cotangent, far_tokens, own_meta, far_meta, lows]
    token_scratch = [VMEM((tokens, half), BF), VMEM((tokens, half), BF), DMA((2,))]
    shapes = [struct((tokens, experts * RANK), BF), struct((experts * capacity, tokens), BF)]
    far_space = pl.ANY
    z, weights, *parts = call(lambda *refs: partial_kernel(full, *refs), shapes + [struct((count, wide), F32) for wide in wides] + [struct((count, wide), BF) for wide in wides], token_args, where, after=early, scratch=token_scratch, spaces=[HBM, far_space, VMEM, VMEM, VMEM])
    kept, sent = (parts[:CHUNKS], parts[CHUNKS:])

    def fold_y(piece, gate):
        group = groups_of[piece][0]
        wide = wides[piece]
        rows = count // (1 + len(group))
        return list(call(lambda keep, *refs: fold_step_kernel(1, keep, *refs), [struct((rows, wide), BF)] * len(group) + [struct((rows, wide), F32)], [kept[piece], swap(sent[piece], 2)], after=gate))
    far = [swap_side(near[0])]
    fold_a = []
    gate = [sent[0], inv_in]
    gate = gate + [far[-1]]
    near[1:] = call(join_kernel, [struct(near[1].shape, BF)], [near[1]], after=gate)
    factors = list(near)
    far.append(swap_side(near[1]))
    factors += [swap(block, 1) for block in near]
    far += [swap(block, 1) for block in far]
    cuts = 2
    scratch = [VMEM((cuts, tokens, half // cuts), BF), VMEM((cuts, experts * RANK, half // cuts), BF), VMEM((cuts, tokens, half // cuts), BF), DMA((cuts, 2 * len(far) + 2))]
    near_coords, delta = call(near_kernel, [struct((experts * RANK, tokens), F32), struct((tokens, width), BF)], [cotangent, z, *factors], where, after=[], scratch=scratch, spaces=[HBM, VMEM] + [HBM] * len(factors), out_spaces=[VMEM, HBM])
    own_rows, far_rows, ends = ([], [], [])
    gates_b = {0: [], 1: [near_coords], 2: [near_coords, far[len(far) // 2 - 1]], 3: [near_coords, far[-1]], 4: [inv_in], 5: [far[len(far) // 2 - 1]], 6: [near_coords, inv_in]}
    folds = [fold_a, fold_y(1, gates_b[2])]
    for piece in range(CHUNKS):
        rows, wide = (count, wides[piece])
        keep = kept[piece]
        for n, group in enumerate(groups_of[piece]):
            radix = 1 + len(group)
            rows //= radix
            if n == 0 and folds[piece]:
                *sends, keep = folds[piece]
            else:
                total = keep
                for more in received if n else [swap(sent[piece], 2)]:
                    total = total + more.astype(F32)
                total = total.reshape(rows // (2 * RANK), radix, 2 * RANK, wide)
                keep = total[:, 0].reshape(rows, wide)
                sends = [total[:, k].reshape(rows, wide).astype(BF) for k in range(1, radix)]
            received = [swap(send, k) for send, k in zip(sends, group)]
        ends.append((keep, received))
        if piece == 0:
            for more in received:
                keep = keep + more.astype(F32)
            own_rows.append(keep[:RANK])
            far_rows.append(swap(keep[RANK:], 1))
    gate_far = [[], [folds[1][-1]], [own_rows[0]], [folds[1][-1], own_rows[0]]][0]
    coords, delta = call(lambda *refs: far_kernel(full, *refs), [struct((experts, RANK, 4 * capacity), BF), struct((tokens, width), BF)], [cotangent, z, weights, near_coords, delta, *far], where, after=gate_far, scratch=scratch, spaces=[HBM, VMEM, VMEM, VMEM, HBM] + [HBM] * len(far), out_spaces=[VMEM, HBM], alias={5: 1})
    keep, received = ends[1]
    keep, send = call(last_fold_kernel, [struct((RANK, wides[1]), F32)] * 2, [keep, *received], after=[coords])
    own_rows.append(keep)
    far_rows.append(swap(send, 1))
    coords = spread(coords)
    pieces = [rows for pair in zip(own_rows, far_rows) for rows in pair]
    scaled_out, = call(scaled_out_kernel, [struct((RANK, width), F32)], [inv_in, *pieces], where, scratch=[VMEM((len(pieces), RANK, max(wides)), F32), DMA((len(pieces),))], out_spaces=[HBM])
    scaled_in, = call(scaled_in_kernel, [struct((RANK, hidden.shape[1]), F32)], [coords, hidden, inv_out])
    return (delta, scaled_in[None], scaled_out[None])


def solution(mesh):
    every = ('group', 'expert')
    return jax.shard_map(on_device, mesh=mesh, in_specs=(P(every, None, None), P('expert', None, None), P('expert', None, None), P(every, None), P(every, None), P(every, None)), out_specs=(P(every, None), P(every, None, None), P(every, None, None)), check_vma=False)
```

```python
import jax
import jax.numpy as jnp
import numpy as np
from jax import lax
from jax.experimental import pallas as pl
from jax.experimental.pallas import tpu as pltpu
from jax.sharding import PartitionSpec as P
BF = jnp.bfloat16
F32 = jnp.float32
HIGHEST = lax.Precision.HIGHEST
RANK = 16
CHUNKS = 2
HBM = pltpu.HBM
VMEM = pltpu.VMEM
DMA = pltpu.SemaphoreType.DMA
MIB = 1024 * 1024

def mm(a, b, ca=1, cb=0, precision=None):
    return lax.dot_general(a, b, (((ca,), (cb,)), ((), ())), preferred_element_type=F32, precision=precision)

def call(kernel, outs, args, scalars=None, after=(), scratch=(), spaces=None, out_spaces=None, alias=None, limit=None):
    size = sum((x.size * x.dtype.itemsize for x in [*args, *outs]))
    total = size + sum((np.prod(x.shape) * x.dtype.itemsize for x in scratch if hasattr(x.dtype, 'itemsize')))
    specs = [pl.BlockSpec(memory_space=space) for space in spaces or [VMEM] * len(args)]
    out_spaces = out_spaces or [VMEM] * len(outs)
    if scalars is not None:
        args = [scalars, *args]
        specs = [pl.BlockSpec(memory_space=pltpu.SMEM), *specs]
    used = len(args)

    def body(*refs):
        kernel(*refs[:used], *refs[used + len(after):])
    return pl.pallas_call(body, out_shape=[jax.ShapeDtypeStruct(o.shape, o.dtype) for o in outs], in_specs=specs + [pl.BlockSpec(memory_space=pl.ANY)] * len(after), out_specs=[pl.BlockSpec(memory_space=space) for space in out_spaces], scratch_shapes=list(scratch), input_output_aliases=alias or {}, compiler_params=pltpu.CompilerParams(vmem_limit_bytes=limit or min(60 * MIB, int(8 * MIB + 1.5 * total))), cost_estimate=pl.CostEstimate(flops=0, bytes_accessed=size, transcendentals=0))(*args, *after)

def split(x):
    high = x.astype(BF)
    return (high, (x - high.astype(F32)).astype(BF))

def lanes(start, size):
    return pl.ds(pl.multiple_of(start, 128), size)

def low_slots_kernel(hidden, a_in, a_out, lows, hidden_in, a_in_in, a_out_in, sems):
    slots = lows.shape[2] // 2
    pieces = 2
    rows = hidden.shape[0] // pieces
    copies = [pltpu.make_async_copy(a_in, a_in_in, sems.at[pieces]), pltpu.make_async_copy(a_out, a_out_in, sems.at[pieces + 1])]
    for i in range(pieces):
        part = pl.ds(i * rows, rows)
        copies.append(pltpu.make_async_copy(hidden.at[part], hidden_in.at[part], sems.at[i]))
    for copy in copies:
        copy.start()
    copies[0].wait()
    copies[1].wait()
    row = lax.broadcasted_iota(jnp.int32, (RANK, slots), 0)
    stats = jnp.zeros((RANK, slots), F32)
    for base, factor in ((0, a_in_in), (3, a_out_in)):
        square = jnp.square(factor[...].astype(F32))
        rest = jnp.sum(jnp.sum(square, axis=1, keepdims=True), axis=0, keepdims=True)
        rest = jnp.broadcast_to(rest, (RANK, slots))
        for piece in range(3):
            part = rest.astype(BF).astype(F32)
            stats = jnp.where(row == base + piece, part, stats)
            rest = rest - part
    stats = stats.astype(BF)
    low = []
    for i in range(pieces):
        copies[2 + i].wait()
        low.append(mm(a_in_in[...], hidden_in[i * rows:(i + 1) * rows, :], 1, 1).astype(BF))
    low = jnp.concatenate(low, axis=1)
    for device in range(lows.shape[0]):
        chip = device // 2
        lows[device, :, 0:slots] = low[:, chip * slots:(chip + 1) * slots]
        lows[device, :, slots:] = stats

def copy_kernel(value, out):
    out[...] = value[...]

def join_kernel(*refs):
    pieces, out = (refs[:-1], refs[-1])
    start = 0
    for piece in pieces:
        out[start:start + piece.shape[0], :] = piece[...]
        start += piece.shape[0]

def fold_of(slots, experts, capacity, source):
    column = lax.broadcasted_iota(jnp.int32, (slots, experts * capacity), 1)
    row = lax.broadcasted_iota(jnp.int32, (slots, experts * capacity), 0)
    return (row == source * capacity + lax.rem(column, capacity)).astype(BF)

def own_expert(experts, capacity):
    shape = (experts * RANK, experts * capacity)
    row = lax.div(lax.broadcasted_iota(jnp.int32, shape, 0), RANK)
    column = lax.div(lax.broadcasted_iota(jnp.int32, shape, 1), capacity)
    return row == column

def relative_experts(order_size, tokens, me):
    row = lax.broadcasted_iota(jnp.int32, (order_size, tokens), 0)
    return jnp.bitwise_xor(row, me).astype(F32)

def weights_of(where, order, own_meta, far_meta, lows, z_out, w_out):
    me, core = (where[0], where[1])
    experts, tokens = (lows.shape[0], own_meta.shape[1])
    slots = lows.shape[2] // 2
    capacity = slots // 2
    low = jnp.concatenate([lows[jnp.bitwise_xor(me, e)][:, 0:slots] for e in range(experts)], axis=0)
    own = own_expert(experts, capacity)
    expert = relative_experts(experts, tokens, me)
    earlier = (lax.broadcasted_iota(jnp.int32, (tokens, tokens), 0) < lax.broadcasted_iota(jnp.int32, (tokens, tokens), 1)).astype(BF)
    place = lax.broadcasted_iota(jnp.int32, (experts, capacity, tokens), 1).astype(F32)
    rows = []
    for s in range(2):
        meta = (own_meta if s == 0 else far_meta)[...].astype(F32)
        first = (meta[0:1] == expert).astype(F32)
        second = (meta[1:2] == expert).astype(F32)
        before = mm((first + second).astype(BF), earlier)
        gate = first * meta[2:3] + second * meta[3:4]
        spread = jnp.where(before[:, None, :] == place, gate[:, None, :], 0.0)
        weights = spread.reshape(experts * capacity, tokens).astype(BF)
        source = jnp.bitwise_xor(core, s)
        wide = mm(low, fold_of(slots, experts, capacity, source))
        wide = jnp.where(own, wide, 0.0).astype(BF)
        exact = mm(wide, weights)
        rows.append(exact.astype(BF))
        if s == 0:
            w_out[...] = weights
            ordered = jnp.concatenate([exact[e * RANK:(e + 1) * RANK] for e in order], axis=0)
            z_out[...] = ordered.T.astype(BF)
    return rows

def product_of(rows, own_in, far_in, here, keep, send):
    count, tokens = (keep.shape[0], rows[0].shape[1])
    groups = rows[0].shape[0] // (4 * RANK)
    for side, target in ((0, keep), (1, send)):
        first, second = (r.reshape(groups, 2, 2 * RANK, tokens)[:, side].reshape(count, tokens) for r in rows)
        total = mm(first, own_in[:, here]) + mm(second, far_in[:, here])
        target[...] = total.astype(target.dtype)

def token_copies(where, cot, packed, own_in, far_in, sems):
    half = own_in.shape[1]
    here = lanes(where[1] * half, half)
    copies = [pltpu.make_async_copy(cot.at[:, here], own_in, sems.at[0])]
    source = packed if packed.shape[1] == half else packed.at[:, here]
    copies.append(pltpu.make_async_copy(source, far_in, sems.at[1]))
    for copy in copies:
        copy.start()
    return copies

def partial_kernel(order, where, cot, packed, own_meta, far_meta, lows, z_out, w_out, *outs):
    keeps, sends = (outs[:CHUNKS], outs[CHUNKS:2 * CHUNKS])
    own_in, far_in, sems = outs[2 * CHUNKS:]
    copies = token_copies(where, cot, packed, own_in, far_in, sems)
    rows = weights_of(where, order, own_meta, far_meta, lows, z_out, w_out)
    for copy in copies:
        copy.wait()
    base = 0
    for keep, send in zip(keeps, sends):
        here = slice(base, base + keep.shape[1])
        base += keep.shape[1]
        product_of(rows, own_in, far_in, here, keep, send)

def fold_step_kernel(received, keep, *refs):
    sends, kept = (refs[received:-1], refs[-1])
    rows, width = keep.shape
    radix = 1 + len(sends)
    total = keep[...]
    for more in refs[:received]:
        total = total + more[...].astype(F32)
    total = total.reshape(rows // (2 * RANK * radix), radix, 2 * RANK, width)
    kept[...] = total[:, 0].reshape(kept.shape)
    for i, send in enumerate(sends):
        send[...] = total[:, i + 1].reshape(send.shape).astype(send.dtype)

def last_fold_kernel(keep, *refs):
    received, (kept, sent) = (refs[:-2], refs[-2:])
    total = keep[...]
    for more in received:
        total = total + more[...].astype(F32)
    kept[...] = total[0:RANK]
    sent[...] = total[RANK:]

def factor_half(flip, side, cot, z, factors, delta, scratch):
    tokens_in, table, result, sems = scratch
    pieces, tokens, cut = tokens_in.shape
    base = jnp.bitwise_xor(side, flip) * (pieces * cut)
    copies = []
    for piece in range(pieces):
        moves = [(cot.at[:, lanes(base + piece * cut, cut)], tokens_in.at[piece])]
        start = 0
        for factor in factors:
            size = factor.shape[0]
            source = factor.at[:, piece * cut:(piece + 1) * cut]
            moves.append((source, table.at[piece, start:start + size, :]))
            start += size
        copies.append([pltpu.make_async_copy(source, target, sems.at[piece, i]) for i, (source, target) in enumerate(moves)])
        for copy in copies[-1]:
            copy.start()
    coords = jnp.zeros((start, tokens), F32)
    writes = []
    for piece in range(pieces):
        for copy in copies[piece]:
            copy.wait()
        block = table[piece]
        result[piece] = mm(z[...], block).astype(BF)
        target = delta.at[:, lanes(base + piece * cut, cut)]
        writes.append(pltpu.make_async_copy(result.at[piece], target, sems.at[piece, len(factors) + 1]))
        writes[-1].start()
        coords = coords + mm(block, tokens_in[piece], 1, 1)
    return (coords, writes)

def near_kernel(where, cot, z, *refs):
    factors, (coords_out, delta), scratch = (refs[:-6], refs[-6:-4], refs[-4:])
    coords_out[...], copies = factor_half(0, where[2], cot, z, factors, delta, scratch)
    for copy in copies:
        copy.wait()

def far_kernel(order, where, cot, z, w, near, _, *refs):
    factors, (coords_out, delta), scratch = (refs[:-6], refs[-6:-4], refs[-4:])
    experts, _, slots = coords_out.shape
    capacity = slots // 4
    coords, copies = factor_half(1, where[2], cot, z, factors, delta, scratch)
    coords = coords + near[...]
    blocks = [order.index(e) * RANK for e in range(experts)]
    coords = jnp.concatenate([coords[b:b + RANK] for b in blocks], axis=0)
    high, low = split(coords)
    picked = mm(high, w[...], 1, 1) + mm(low, w[...], 1, 1)
    picked = jnp.where(own_expert(experts, capacity), picked, 0.0).astype(BF)
    fold = fold_of(slots, experts, capacity, lax.rem(where[0], 4))
    rows = mm(picked, fold, 1, 1).astype(coords_out.dtype)
    for e in range(experts):
        coords_out[jnp.bitwise_xor(where[0], e)] = rows[e * RANK:(e + 1) * RANK]
    for copy in copies:
        copy.wait()

def inverse_kernel(a_in, a_out, lows, inv_in, inv_out):
    experts, _, double = lows.shape
    stats = jnp.sum(lows[:, :, double // 2:].astype(F32), axis=0)
    row = lax.broadcasted_iota(jnp.int32, (RANK, RANK), 0)
    column = lax.broadcasted_iota(jnp.int32, (RANK, RANK), 1)
    eye = (row == column).astype(F32)
    works = []
    for base, factor in ((0, a_in), (3, a_out)):
        pieces = stats[base:base + 1, 0:1] + stats[base + 1:base + 2, 0:1]
        damp = (pieces + stats[base + 2:base + 3, 0:1]) / (float(RANK) * experts)
        gram = mm(factor[...], factor[...], 1, 1) + damp * eye
        works.append([gram, eye])
    for j in range(RANK):
        for work in works:
            gram, inverse = work
            pivot = 1.0 / gram[j:j + 1, j:j + 1]
            gram_row, inverse_row = (gram[j:j + 1] * pivot, inverse[j:j + 1] * pivot)
            scale = gram[:, j:j + 1]
            work[0] = jnp.where(row == j, gram_row, gram - scale * gram_row)
            work[1] = jnp.where(row == j, inverse_row, inverse - scale * inverse_row)
    inv_in[...] = works[0][1]
    inv_out[...] = works[1][1]

def scaled_in_kernel(coords, hidden, inverse, out):
    pieces = []
    for base in range(0, coords.shape[0], 4):
        total = coords[base].astype(F32)
        for q in range(1, 4):
            total = total + coords[base + q].astype(F32)
        pieces.append(total)
    grad_low = jnp.concatenate(pieces, axis=1).astype(BF)
    out[...] = mm(inverse[...], mm(grad_low, hidden[...]), precision=HIGHEST)

def scaled_out_kernel(where, inverse, *refs):
    pieces, (out, rows, sems) = (refs[:-3], refs[-3:])
    half = out.shape[1] // 2
    copies, starts = ([], [0, 0])
    for i, piece in enumerate(pieces):
        flip, width = (i % 2, piece.shape[1])
        base = jnp.bitwise_xor(where[1], flip) * half + starts[flip]
        starts[flip] += width
        rows[i, :, 0:width] = mm(inverse[...], piece[...], precision=HIGHEST)
        target = out.at[:, lanes(base, width)]
        copies.append(pltpu.make_async_copy(rows.at[i, :, 0:width], target, sems.at[i]))
        copies[-1].start()
    for copy in copies:
        copy.wait()

def radix_groups(experts):
    groups, bit = ([], 4)
    while bit < experts:
        radix = min(4, experts // bit)
        groups.append([bit * k for k in range(1, radix)])
        bit *= radix
    return groups

def relative_order(bits):
    order = [0]
    for bit in bits:
        order = order + [e ^ bit for e in order]
    return order

def on_device(hidden_slots, adapter_in, adapter_out, expert_ids, gate_weights, cotangent):
    experts, groups = (lax.axis_size('expert'), lax.axis_size('group'))
    me, group = (lax.axis_index('expert'), lax.axis_index('group'))
    where = jnp.stack([me, me % 2, group % 2]).astype(jnp.int32)
    hidden, a_in, a_out = (hidden_slots[0], adapter_in[0], adapter_out[0])
    width = a_out.shape[1]
    half = width // 2
    tokens = cotangent.shape[0]
    capacity = hidden.shape[0] // experts
    struct = jax.ShapeDtypeStruct

    def swap(x, bit):
        return lax.ppermute(x, 'expert', [(i, i ^ bit) for i in range(experts)])

    def swap_side(x):
        return lax.ppermute(x, 'group', [(i, i ^ 1) for i in range(groups)])

    def spread(x):
        return lax.all_to_all(x, 'expert', split_axis=0, concat_axis=0, tiled=True)
    groups_z = radix_groups(experts)
    far_bits = [1 << i for i in reversed(range(2, experts.bit_length() - 1))]
    full = relative_order([2, *far_bits, 1])
    block = lax.dynamic_slice_in_dim(a_out, group % 2 * half, half, axis=1)
    received = swap(block, 2)
    low, = call(low_slots_kernel, [struct((experts, RANK, 4 * capacity), BF)], [hidden, a_in, a_out], scratch=[VMEM(hidden.shape, BF), VMEM(a_in.shape, BF), VMEM(a_out.shape, BF), DMA((2 + 2,))], spaces=[HBM] * 3, limit=63 * MIB)
    far_tokens = swap(cotangent, 1)
    own_meta = jnp.concatenate([expert_ids.T.astype(BF), gate_weights.T.astype(BF), jnp.zeros((12, tokens), BF)], axis=0)
    far_meta = swap(own_meta, 1)
    block, = call(join_kernel, [struct((2 * RANK, half), BF)], [block, received], after=[low])
    lows, = call(copy_kernel, [low], [low], after=[block])
    lows = spread(lows)
    inv_in, inv_out = call(inverse_kernel, [struct((RANK, RANK), F32)] * 2, [a_in, a_out, lows])
    count = experts * RANK // 2

    def planes_of(block, gate):
        pieces = block
        for bit in far_bits:
            if bit == far_bits[-1]:
                return ([block, swap(block, bit)], last)
            last = pieces + [swap(piece, bit) for piece in pieces]
            block, = call(join_kernel, [struct((2 * sum((piece.shape[0] for piece in pieces)), half), BF)], last, after=gate)
            pieces = [block]
    near, last = planes_of([block], [lows])
    tiles = half // 128
    wides = [128 * (tiles // 2), half - 128 * (tiles // 2)]
    token_args = [cotangent, far_tokens, own_meta, far_meta, lows]
    token_scratch = [VMEM((tokens, half), BF), VMEM((tokens, half), BF), DMA((2,))]
    shapes = [struct((tokens, experts * RANK), BF), struct((experts * capacity, tokens), BF)]
    z, weights, *parts = call(lambda *refs: partial_kernel(full, *refs), shapes + [struct((count, wide), F32) for wide in wides] + [struct((count, wide), BF) for wide in wides], token_args, where, after=[near[0]], scratch=token_scratch, spaces=[HBM, pl.ANY, VMEM, VMEM, VMEM])
    kept, sent = (parts[:CHUNKS], parts[CHUNKS:])

    def fold_y(piece, gate):
        group = groups_z[0]
        wide = wides[piece]
        rows = count // (1 + len(group))
        return list(call(lambda keep, *refs: fold_step_kernel(1, keep, *refs), [struct((rows, wide), BF)] * len(group) + [struct((rows, wide), F32)], [kept[piece], swap(sent[piece], 2)], after=gate))
    far = [swap_side(near[0])]
    near[1:] = call(join_kernel, [struct(near[1].shape, BF)], [near[1]], after=[sent[0], inv_in, far[0]])
    factors = list(near)
    far.append(swap_side(near[1]))
    factors += [swap(block, 1) for block in near]
    far += [swap(block, 1) for block in far]
    cuts = 2
    scratch = [VMEM((cuts, tokens, half // cuts), BF), VMEM((cuts, experts * RANK, half // cuts), BF), VMEM((cuts, tokens, half // cuts), BF), DMA((cuts, 2 * len(far) + 2))]
    near_coords, delta = call(near_kernel, [struct((experts * RANK, tokens), F32), struct((tokens, width), BF)], [cotangent, z, *factors], where, scratch=scratch, spaces=[HBM, VMEM] + [HBM] * len(factors), out_spaces=[VMEM, HBM])
    own_rows, far_rows, ends = ([], [], [])
    folds = [None, fold_y(1, [near_coords, far[1]])]
    for piece in range(CHUNKS):
        rows, wide = (count, wides[piece])
        keep = kept[piece]
        for n, group in enumerate(groups_z):
            radix = 1 + len(group)
            rows //= radix
            if n == 0 and folds[piece]:
                *sends, keep = folds[piece]
            else:
                total = keep
                for more in received if n else [swap(sent[piece], 2)]:
                    total = total + more.astype(F32)
                total = total.reshape(rows // (2 * RANK), radix, 2 * RANK, wide)
                keep = total[:, 0].reshape(rows, wide)
                sends = [total[:, k].reshape(rows, wide).astype(BF) for k in range(1, radix)]
            received = [swap(send, k) for send, k in zip(sends, group)]
        ends.append((keep, received))
        if piece == 0:
            for more in received:
                keep = keep + more.astype(F32)
            own_rows.append(keep[:RANK])
            far_rows.append(swap(keep[RANK:], 1))
    coords, delta = call(lambda *refs: far_kernel(full, *refs), [struct((experts, RANK, 4 * capacity), BF), struct((tokens, width), BF)], [cotangent, z, weights, near_coords, delta, *far], where, scratch=scratch, spaces=[HBM, VMEM, VMEM, VMEM, HBM] + [HBM] * len(far), out_spaces=[VMEM, HBM], alias={5: 1})
    keep, received = ends[1]
    keep, send = call(last_fold_kernel, [struct((RANK, wides[1]), F32)] * 2, [keep, *received], after=[coords])
    own_rows.append(keep)
    far_rows.append(swap(send, 1))
    coords = spread(coords)
    pieces = [rows for pair in zip(own_rows, far_rows) for rows in pair]
    scaled_out, = call(scaled_out_kernel, [struct((RANK, width), F32)], [inv_in, *pieces], where, scratch=[VMEM((len(pieces), RANK, max(wides)), F32), DMA((len(pieces),))], out_spaces=[HBM])
    scaled_in, = call(scaled_in_kernel, [struct((RANK, hidden.shape[1]), F32)], [coords, hidden, inv_out])
    return (delta, scaled_in[None], scaled_out[None])

def solution(mesh):
    every = ('group', 'expert')
    return jax.shard_map(on_device, mesh=mesh, in_specs=(P(every, None, None), P('expert', None, None), P('expert', None, None), P(every, None), P(every, None), P(every, None)), out_specs=(P(every, None), P(every, None, None), P(every, None, None)), check_vma=False)
```

```python
import jax
import jax.numpy as jnp
import numpy as np
from jax import lax
from jax.experimental import pallas as pl
from jax.experimental.pallas import tpu as pltpu
from jax.sharding import PartitionSpec as P
BF = jnp.bfloat16
F32 = jnp.float32
HIGHEST = lax.Precision.HIGHEST
RANK = 16
CHUNKS = 2
HBM = pltpu.HBM
VMEM = pltpu.VMEM
DMA = pltpu.SemaphoreType.DMA
MIB = 1024 * 1024

def mm(a, b, ca=1, cb=0, precision=None):
    return lax.dot_general(a, b, (((ca,), (cb,)), ((), ())), preferred_element_type=F32, precision=precision)

def call(kernel, outs, args, scalars=None, after=(), scratch=(), spaces=None, out_spaces=None, alias=None, limit=None):
    size = sum((x.size * x.dtype.itemsize for x in [*args, *outs]))
    total = size + sum((np.prod(x.shape) * x.dtype.itemsize for x in scratch if hasattr(x.dtype, 'itemsize')))
    specs = [pl.BlockSpec(memory_space=space) for space in spaces or [VMEM] * len(args)]
    out_spaces = out_spaces or [VMEM] * len(outs)
    if scalars is not None:
        args = [scalars, *args]
        specs = [pl.BlockSpec(memory_space=pltpu.SMEM), *specs]
    used = len(args)

    def body(*refs):
        kernel(*refs[:used], *refs[used + len(after):])
    return pl.pallas_call(body, out_shape=[jax.ShapeDtypeStruct(o.shape, o.dtype) for o in outs], in_specs=specs + [pl.BlockSpec(memory_space=pl.ANY)] * len(after), out_specs=[pl.BlockSpec(memory_space=space) for space in out_spaces], scratch_shapes=list(scratch), input_output_aliases=alias or {}, compiler_params=pltpu.CompilerParams(vmem_limit_bytes=limit or min(60 * MIB, int(8 * MIB + 1.5 * total))), cost_estimate=pl.CostEstimate(flops=0, bytes_accessed=size, transcendentals=0))(*args, *after)

def split(x):
    high = x.astype(BF)
    return (high, (x - high.astype(F32)).astype(BF))

def lanes(start, size):
    return pl.ds(pl.multiple_of(start, 128), size)

def low_slots_kernel(hidden, a_in, a_out, lows, hidden_in, a_in_in, a_out_in, sems):
    slots = lows.shape[2] // 2
    pieces = 2
    rows = hidden.shape[0] // pieces
    copies = [pltpu.make_async_copy(a_in, a_in_in, sems.at[pieces]), pltpu.make_async_copy(a_out, a_out_in, sems.at[pieces + 1])]
    for i in range(pieces):
        part = pl.ds(i * rows, rows)
        copies.append(pltpu.make_async_copy(hidden.at[part], hidden_in.at[part], sems.at[i]))
    for copy in copies:
        copy.start()
    copies[0].wait()
    copies[1].wait()
    row = lax.broadcasted_iota(jnp.int32, (RANK, slots), 0)
    stats = jnp.zeros((RANK, slots), F32)
    for base, factor in ((0, a_in_in), (3, a_out_in)):
        square = jnp.square(factor[...].astype(F32))
        rest = jnp.sum(jnp.sum(square, axis=1, keepdims=True), axis=0, keepdims=True)
        rest = jnp.broadcast_to(rest, (RANK, slots))
        for piece in range(3):
            part = rest.astype(BF).astype(F32)
            stats = jnp.where(row == base + piece, part, stats)
            rest = rest - part
    stats = stats.astype(BF)
    low = []
    for i in range(pieces):
        copies[2 + i].wait()
        low.append(mm(a_in_in[...], hidden_in[i * rows:(i + 1) * rows, :], 1, 1).astype(BF))
    low = jnp.concatenate(low, axis=1)
    for device in range(lows.shape[0]):
        chip = device // 2
        lows[device, :, 0:slots] = low[:, chip * slots:(chip + 1) * slots]
        lows[device, :, slots:] = stats

def copy_kernel(value, out):
    out[...] = value[...]

def join_kernel(*refs):
    pieces, out = (refs[:-1], refs[-1])
    start = 0
    for piece in pieces:
        out[start:start + piece.shape[0], :] = piece[...]
        start += piece.shape[0]

def fold_of(slots, experts, capacity, source):
    column = lax.broadcasted_iota(jnp.int32, (slots, experts * capacity), 1)
    row = lax.broadcasted_iota(jnp.int32, (slots, experts * capacity), 0)
    return (row == source * capacity + lax.rem(column, capacity)).astype(BF)

def own_expert(experts, capacity):
    shape = (experts * RANK, experts * capacity)
    row = lax.div(lax.broadcasted_iota(jnp.int32, shape, 0), RANK)
    column = lax.div(lax.broadcasted_iota(jnp.int32, shape, 1), capacity)
    return row == column

def relative_experts(order_size, tokens, me):
    row = lax.broadcasted_iota(jnp.int32, (order_size, tokens), 0)
    return jnp.bitwise_xor(row, me).astype(F32)

def weights_of(where, order, own_meta, far_meta, lows, z_out, w_out):
    me, core = (where[0], where[1])
    experts, tokens = (lows.shape[0], own_meta.shape[1])
    slots = lows.shape[2] // 2
    capacity = slots // 2
    low = jnp.concatenate([lows[jnp.bitwise_xor(me, e)][:, 0:slots] for e in range(experts)], axis=0)
    own = own_expert(experts, capacity)
    expert = relative_experts(experts, tokens, me)
    earlier = (lax.broadcasted_iota(jnp.int32, (tokens, tokens), 0) < lax.broadcasted_iota(jnp.int32, (tokens, tokens), 1)).astype(BF)
    place = lax.broadcasted_iota(jnp.int32, (experts, capacity, tokens), 1).astype(F32)
    rows = []
    for s in range(2):
        meta = (own_meta if s == 0 else far_meta)[...].astype(F32)
        first = (meta[0:1] == expert).astype(F32)
        second = (meta[1:2] == expert).astype(F32)
        before = mm((first + second).astype(BF), earlier)
        gate = first * meta[2:3] + second * meta[3:4]
        spread = jnp.where(before[:, None, :] == place, gate[:, None, :], 0.0)
        weights = spread.reshape(experts * capacity, tokens).astype(BF)
        source = jnp.bitwise_xor(core, s)
        wide = mm(low, fold_of(slots, experts, capacity, source))
        wide = jnp.where(own, wide, 0.0).astype(BF)
        exact = mm(wide, weights)
        rows.append(exact.astype(BF))
        if s == 0:
            w_out[...] = weights
            ordered = jnp.concatenate([exact[e * RANK:(e + 1) * RANK] for e in order], axis=0)
            z_out[...] = ordered.T.astype(BF)
    return rows

def product_of(rows, tokens_in, here, keep, send):
    count = keep.shape[0]
    total = mm(rows, tokens_in[:, here])
    keep[...] = total[0:count]
    send[...] = total[count:].astype(send.dtype)

def token_copies(where, cot, packed, tokens_in, sems):
    half, tokens = tokens_in.shape[1], cot.shape[0]
    here = lanes(where[1] * half, half)
    copies = [
        pltpu.make_async_copy(cot.at[:, here], tokens_in.at[0:tokens, :], sems.at[0]),
        pltpu.make_async_copy(packed.at[:, here], tokens_in.at[tokens : 2 * tokens, :], sems.at[1]),
    ]
    for copy in copies:
        copy.start()
    return copies

def partial_kernel(order, where, cot, packed, own_meta, far_meta, lows, z_out, w_out, *outs):
    keeps, sends = outs[:CHUNKS], outs[CHUNKS : 2 * CHUNKS]
    tokens_in, sems = outs[2 * CHUNKS :]
    copies = token_copies(where, cot, packed, tokens_in, sems)
    rows = weights_of(where, order, own_meta, far_meta, lows, z_out, w_out)
    rows = jnp.concatenate(rows, axis=1)
    count, depth = keeps[0].shape[0], rows.shape[1]
    rows = rows.reshape(count // (2 * RANK), 2, 2 * RANK, depth)
    rows = jnp.concatenate([rows[:, side].reshape(count, depth) for side in range(2)], axis=0)
    for copy in copies:
        copy.wait()
    base = 0
    for keep, send in zip(keeps, sends):
        here = slice(base, base + keep.shape[1])
        base += keep.shape[1]
        product_of(rows, tokens_in, here, keep, send)

def fold_step_kernel(received, keep, *refs):
    sends, kept = (refs[received:-1], refs[-1])
    rows, width = keep.shape
    radix = 1 + len(sends)
    total = keep[...]
    for more in refs[:received]:
        total = total + more[...].astype(F32)
    total = total.reshape(rows // (2 * RANK * radix), radix, 2 * RANK, width)
    kept[...] = total[:, 0].reshape(kept.shape)
    for i, send in enumerate(sends):
        send[...] = total[:, i + 1].reshape(send.shape).astype(send.dtype)

def last_fold_kernel(keep, *refs):
    received, (kept, sent) = (refs[:-2], refs[-2:])
    total = keep[...]
    for more in received:
        total = total + more[...].astype(F32)
    kept[...] = total[0:RANK]
    sent[...] = total[RANK:]

def factor_half(flip, side, cot, z, factors, delta, scratch):
    tokens_in, table, result, sems = scratch
    pieces, tokens, cut = tokens_in.shape
    base = jnp.bitwise_xor(side, flip) * (pieces * cut)
    copies = []
    for piece in range(pieces):
        moves = [(cot.at[:, lanes(base + piece * cut, cut)], tokens_in.at[piece])]
        start = 0
        for factor in factors:
            size = factor.shape[0]
            source = factor.at[:, piece * cut:(piece + 1) * cut]
            moves.append((source, table.at[piece, start:start + size, :]))
            start += size
        copies.append([pltpu.make_async_copy(source, target, sems.at[piece, i]) for i, (source, target) in enumerate(moves)])
        for copy in copies[-1]:
            copy.start()
    coords = jnp.zeros((start, tokens), F32)
    writes = []
    for piece in range(pieces):
        for copy in copies[piece]:
            copy.wait()
        block = table[piece]
        result[piece] = mm(z[...], block).astype(BF)
        target = delta.at[:, lanes(base + piece * cut, cut)]
        writes.append(pltpu.make_async_copy(result.at[piece], target, sems.at[piece, len(factors) + 1]))
        writes[-1].start()
        coords = coords + mm(block, tokens_in[piece], 1, 1)
    return (coords, writes)

def near_kernel(where, cot, z, *refs):
    factors, (coords_out, delta), scratch = (refs[:-6], refs[-6:-4], refs[-4:])
    coords_out[...], copies = factor_half(0, where[2], cot, z, factors, delta, scratch)
    for copy in copies:
        copy.wait()

def far_kernel(order, where, cot, z, w, near, _, *refs):
    factors, (coords_out, delta), scratch = (refs[:-6], refs[-6:-4], refs[-4:])
    experts, _, slots = coords_out.shape
    capacity = slots // 4
    coords, copies = factor_half(1, where[2], cot, z, factors, delta, scratch)
    coords = coords + near[...]
    blocks = [order.index(e) * RANK for e in range(experts)]
    coords = jnp.concatenate([coords[b:b + RANK] for b in blocks], axis=0)
    high, low = split(coords)
    picked = mm(high, w[...], 1, 1) + mm(low, w[...], 1, 1)
    picked = jnp.where(own_expert(experts, capacity), picked, 0.0).astype(BF)
    fold = fold_of(slots, experts, capacity, lax.rem(where[0], 4))
    rows = mm(picked, fold, 1, 1).astype(coords_out.dtype)
    for e in range(experts):
        coords_out[jnp.bitwise_xor(where[0], e)] = rows[e * RANK:(e + 1) * RANK]
    for copy in copies:
        copy.wait()

def inverse_kernel(a_in, a_out, lows, inv_in, inv_out):
    experts, _, double = lows.shape
    stats = jnp.sum(lows[:, :, double // 2:].astype(F32), axis=0)
    row = lax.broadcasted_iota(jnp.int32, (RANK, RANK), 0)
    column = lax.broadcasted_iota(jnp.int32, (RANK, RANK), 1)
    eye = (row == column).astype(F32)
    works = []
    for base, factor in ((0, a_in), (3, a_out)):
        pieces = stats[base:base + 1, 0:1] + stats[base + 1:base + 2, 0:1]
        damp = (pieces + stats[base + 2:base + 3, 0:1]) / (float(RANK) * experts)
        gram = mm(factor[...], factor[...], 1, 1) + damp * eye
        works.append([gram, eye])
    for j in range(RANK):
        for work in works:
            gram, inverse = work
            pivot = 1.0 / gram[j:j + 1, j:j + 1]
            gram_row, inverse_row = (gram[j:j + 1] * pivot, inverse[j:j + 1] * pivot)
            scale = gram[:, j:j + 1]
            work[0] = jnp.where(row == j, gram_row, gram - scale * gram_row)
            work[1] = jnp.where(row == j, inverse_row, inverse - scale * inverse_row)
    inv_in[...] = works[0][1]
    inv_out[...] = works[1][1]

def scaled_in_kernel(coords, hidden, inverse, out):
    pieces = []
    for base in range(0, coords.shape[0], 4):
        total = coords[base].astype(F32)
        for q in range(1, 4):
            total = total + coords[base + q].astype(F32)
        pieces.append(total)
    grad_low = jnp.concatenate(pieces, axis=1).astype(BF)
    out[...] = mm(inverse[...], mm(grad_low, hidden[...]), precision=HIGHEST)

def scaled_out_kernel(where, inverse, *refs):
    pieces, (out, rows, sems) = (refs[:-3], refs[-3:])
    half = out.shape[1] // 2
    copies, starts = ([], [0, 0])
    for i, piece in enumerate(pieces):
        flip, width = (i % 2, piece.shape[1])
        base = jnp.bitwise_xor(where[1], flip) * half + starts[flip]
        starts[flip] += width
        rows[i, :, 0:width] = mm(inverse[...], piece[...], precision=HIGHEST)
        target = out.at[:, lanes(base, width)]
        copies.append(pltpu.make_async_copy(rows.at[i, :, 0:width], target, sems.at[i]))
        copies[-1].start()
    for copy in copies:
        copy.wait()

def radix_groups(experts):
    groups, bit = ([], 4)
    while bit < experts:
        radix = min(4, experts // bit)
        groups.append([bit * k for k in range(1, radix)])
        bit *= radix
    return groups

def relative_order(bits):
    order = [0]
    for bit in bits:
        order = order + [e ^ bit for e in order]
    return order

def on_device(hidden_slots, adapter_in, adapter_out, expert_ids, gate_weights, cotangent):
    experts, groups = (lax.axis_size('expert'), lax.axis_size('group'))
    me, group = (lax.axis_index('expert'), lax.axis_index('group'))
    where = jnp.stack([me, me % 2, group % 2]).astype(jnp.int32)
    hidden, a_in, a_out = (hidden_slots[0], adapter_in[0], adapter_out[0])
    width = a_out.shape[1]
    half = width // 2
    tokens = cotangent.shape[0]
    capacity = hidden.shape[0] // experts
    struct = jax.ShapeDtypeStruct

    def swap(x, bit):
        return lax.ppermute(x, 'expert', [(i, i ^ bit) for i in range(experts)])

    def swap_side(x):
        return lax.ppermute(x, 'group', [(i, i ^ 1) for i in range(groups)])

    def spread(x):
        return lax.all_to_all(x, 'expert', split_axis=0, concat_axis=0, tiled=True)
    groups_z = radix_groups(experts)
    far_bits = [1 << i for i in reversed(range(2, experts.bit_length() - 1))]
    full = relative_order([2, *far_bits, 1])
    block = lax.dynamic_slice_in_dim(a_out, group % 2 * half, half, axis=1)
    received = swap(block, 2)
    low, = call(low_slots_kernel, [struct((experts, RANK, 4 * capacity), BF)], [hidden, a_in, a_out], scratch=[VMEM(hidden.shape, BF), VMEM(a_in.shape, BF), VMEM(a_out.shape, BF), DMA((2 + 2,))], spaces=[HBM] * 3, limit=63 * MIB)
    far_tokens = swap(cotangent, 1)
    own_meta = jnp.concatenate([expert_ids.T.astype(BF), gate_weights.T.astype(BF), jnp.zeros((12, tokens), BF)], axis=0)
    far_meta = swap(own_meta, 1)
    block, = call(join_kernel, [struct((2 * RANK, half), BF)], [block, received], after=[low])
    lows, = call(copy_kernel, [low], [low], after=[block])
    lows = spread(lows)
    inv_in, inv_out = call(inverse_kernel, [struct((RANK, RANK), F32)] * 2, [a_in, a_out, lows])
    count = experts * RANK // 2

    def planes_of(block, gate):
        pieces = block
        for bit in far_bits:
            if bit == far_bits[-1]:
                return ([block, swap(block, bit)], last)
            last = pieces + [swap(piece, bit) for piece in pieces]
            block, = call(join_kernel, [struct((2 * sum((piece.shape[0] for piece in pieces)), half), BF)], last, after=gate)
            pieces = [block]
    near, last = planes_of([block], [lows])
    tiles = half // 128
    wides = [128 * (tiles // 2), half - 128 * (tiles // 2)]
    token_args = [cotangent, far_tokens, own_meta, far_meta, lows]
    token_scratch = [VMEM((2 * tokens, half), BF), DMA((2,))]
    shapes = [struct((tokens, experts * RANK), BF), struct((experts * capacity, tokens), BF)]
    z, weights, *parts = call(lambda *refs: partial_kernel(full, *refs), shapes + [struct((count, wide), F32) for wide in wides] + [struct((count, wide), BF) for wide in wides], token_args, where, after=[near[0]], scratch=token_scratch, spaces=[HBM, pl.ANY, VMEM, VMEM, VMEM])
    kept, sent = (parts[:CHUNKS], parts[CHUNKS:])

    def fold_y(piece, gate):
        group = groups_z[0]
        wide = wides[piece]
        rows = count // (1 + len(group))
        return list(call(lambda keep, *refs: fold_step_kernel(1, keep, *refs), [struct((rows, wide), BF)] * len(group) + [struct((rows, wide), F32)], [kept[piece], swap(sent[piece], 2)], after=gate))
    far = [swap_side(near[0])]
    near[1:] = call(join_kernel, [struct(near[1].shape, BF)], [near[1]], after=[sent[0], inv_in, far[0]])
    factors = list(near)
    far.append(swap_side(near[1]))
    factors += [swap(block, 1) for block in near]
    far += [swap(block, 1) for block in far]
    cuts = 2
    scratch = [VMEM((cuts, tokens, half // cuts), BF), VMEM((cuts, experts * RANK, half // cuts), BF), VMEM((cuts, tokens, half // cuts), BF), DMA((cuts, 2 * len(far) + 2))]
    near_coords, delta = call(near_kernel, [struct((experts * RANK, tokens), F32), struct((tokens, width), BF)], [cotangent, z, *factors], where, scratch=scratch, spaces=[HBM, VMEM] + [HBM] * len(factors), out_spaces=[VMEM, HBM])
    own_rows, far_rows, ends = ([], [], [])
    folds = [None, fold_y(1, [near_coords, far[1]])]
    for piece in range(CHUNKS):
        rows, wide = (count, wides[piece])
        keep = kept[piece]
        for n, group in enumerate(groups_z):
            radix = 1 + len(group)
            rows //= radix
            if n == 0 and folds[piece]:
                *sends, keep = folds[piece]
            else:
                total = keep
                for more in received if n else [swap(sent[piece], 2)]:
                    total = total + more.astype(F32)
                total = total.reshape(rows // (2 * RANK), radix, 2 * RANK, wide)
                keep = total[:, 0].reshape(rows, wide)
                sends = [total[:, k].reshape(rows, wide).astype(BF) for k in range(1, radix)]
            received = [swap(send, k) for send, k in zip(sends, group)]
        ends.append((keep, received))
        if piece == 0:
            for more in received:
                keep = keep + more.astype(F32)
            own_rows.append(keep[:RANK])
            far_rows.append(swap(keep[RANK:], 1))
    coords, delta = call(lambda *refs: far_kernel(full, *refs), [struct((experts, RANK, 4 * capacity), BF), struct((tokens, width), BF)], [cotangent, z, weights, near_coords, delta, *far], where, scratch=scratch, spaces=[HBM, VMEM, VMEM, VMEM, HBM] + [HBM] * len(far), out_spaces=[VMEM, HBM], alias={5: 1})
    keep, received = ends[1]
    keep, send = call(last_fold_kernel, [struct((RANK, wides[1]), F32)] * 2, [keep, *received], after=[coords])
    own_rows.append(keep)
    far_rows.append(swap(send, 1))
    coords = spread(coords)
    pieces = [rows for pair in zip(own_rows, far_rows) for rows in pair]
    scaled_out, = call(scaled_out_kernel, [struct((RANK, width), F32)], [inv_in, *pieces], where, scratch=[VMEM((len(pieces), RANK, max(wides)), F32), DMA((len(pieces),))], out_spaces=[HBM])
    scaled_in, = call(scaled_in_kernel, [struct((RANK, hidden.shape[1]), F32)], [coords, hidden, inv_out])
    return (delta, scaled_in[None], scaled_out[None])

def solution(mesh):
    every = ('group', 'expert')
    return jax.shard_map(on_device, mesh=mesh, in_specs=(P(every, None, None), P('expert', None, None), P('expert', None, None), P(every, None), P(every, None), P(every, None)), out_specs=(P(every, None), P(every, None, None), P(every, None, None)), check_vma=False)
```

```python
import jax
import jax.numpy as jnp
import numpy as np
from jax import lax
from jax.experimental import pallas as pl
from jax.experimental.pallas import tpu as pltpu
from jax.sharding import PartitionSpec as P
BF = jnp.bfloat16
F32 = jnp.float32
HIGHEST = lax.Precision.HIGHEST
RANK = 16
CHUNKS = 2
HBM = pltpu.HBM
VMEM = pltpu.VMEM
DMA = pltpu.SemaphoreType.DMA
MIB = 1024 * 1024

def mm(a, b, ca=1, cb=0, precision=None):
    return lax.dot_general(a, b, (((ca,), (cb,)), ((), ())), preferred_element_type=F32, precision=precision)

def call(kernel, outs, args, scalars=None, after=(), scratch=(), spaces=None, out_spaces=None, alias=None, limit=None):
    size = sum((x.size * x.dtype.itemsize for x in [*args, *outs]))
    total = size + sum((np.prod(x.shape) * x.dtype.itemsize for x in scratch if hasattr(x.dtype, 'itemsize')))
    specs = [pl.BlockSpec(memory_space=space) for space in spaces or [VMEM] * len(args)]
    out_spaces = out_spaces or [VMEM] * len(outs)
    if scalars is not None:
        args = [scalars, *args]
        specs = [pl.BlockSpec(memory_space=pltpu.SMEM), *specs]
    used = len(args)

    def body(*refs):
        kernel(*refs[:used], *refs[used + len(after):])
    return pl.pallas_call(body, out_shape=[jax.ShapeDtypeStruct(o.shape, o.dtype) for o in outs], in_specs=specs + [pl.BlockSpec(memory_space=pl.ANY)] * len(after), out_specs=[pl.BlockSpec(memory_space=space) for space in out_spaces], scratch_shapes=list(scratch), input_output_aliases=alias or {}, compiler_params=pltpu.CompilerParams(vmem_limit_bytes=limit or min(60 * MIB, int(8 * MIB + 1.5 * total))), cost_estimate=pl.CostEstimate(flops=0, bytes_accessed=size, transcendentals=0))(*args, *after)

def split(x):
    high = x.astype(BF)
    return (high, (x - high.astype(F32)).astype(BF))

def lanes(start, size):
    return pl.ds(pl.multiple_of(start, 128), size)

def low_slots_kernel(hidden, a_in, a_out, lows, hidden_in, a_in_in, a_out_in, sems):
    slots = lows.shape[2] // 2
    pieces = 2
    rows = hidden.shape[0] // pieces
    copies = [pltpu.make_async_copy(a_in, a_in_in, sems.at[pieces]), pltpu.make_async_copy(a_out, a_out_in, sems.at[pieces + 1])]
    for i in range(pieces):
        part = pl.ds(i * rows, rows)
        copies.append(pltpu.make_async_copy(hidden.at[part], hidden_in.at[part], sems.at[i]))
    for copy in copies:
        copy.start()
    copies[0].wait()
    copies[1].wait()
    row = lax.broadcasted_iota(jnp.int32, (RANK, slots), 0)
    stats = jnp.zeros((RANK, slots), F32)
    for base, factor in ((0, a_in_in), (3, a_out_in)):
        square = jnp.square(factor[...].astype(F32))
        rest = jnp.sum(jnp.sum(square, axis=1, keepdims=True), axis=0, keepdims=True)
        rest = jnp.broadcast_to(rest, (RANK, slots))
        for piece in range(3):
            part = rest.astype(BF).astype(F32)
            stats = jnp.where(row == base + piece, part, stats)
            rest = rest - part
    stats = stats.astype(BF)
    low = []
    for i in range(pieces):
        copies[2 + i].wait()
        low.append(mm(a_in_in[...], hidden_in[i * rows:(i + 1) * rows, :], 1, 1).astype(BF))
    low = jnp.concatenate(low, axis=1)
    for device in range(lows.shape[0]):
        chip = device // 2
        lows[device, :, 0:slots] = low[:, chip * slots:(chip + 1) * slots]
        lows[device, :, slots:] = stats

def copy_kernel(value, out):
    out[...] = value[...]

def join_kernel(*refs):
    pieces, out = (refs[:-1], refs[-1])
    start = 0
    for piece in pieces:
        out[start:start + piece.shape[0], :] = piece[...]
        start += piece.shape[0]

def fold_of(slots, experts, capacity, source):
    column = lax.broadcasted_iota(jnp.int32, (slots, experts * capacity), 1)
    row = lax.broadcasted_iota(jnp.int32, (slots, experts * capacity), 0)
    return (row == source * capacity + lax.rem(column, capacity)).astype(BF)

def own_expert(experts, capacity):
    shape = (experts * RANK, experts * capacity)
    row = lax.div(lax.broadcasted_iota(jnp.int32, shape, 0), RANK)
    column = lax.div(lax.broadcasted_iota(jnp.int32, shape, 1), capacity)
    return row == column

def relative_experts(order_size, tokens, me):
    row = lax.broadcasted_iota(jnp.int32, (order_size, tokens), 0)
    return jnp.bitwise_xor(row, me).astype(F32)

def weights_of(where, order, own_meta, far_meta, lows, z_out, w_out):
    me, core = (where[0], where[1])
    experts, tokens = (lows.shape[0], own_meta.shape[1])
    slots = lows.shape[2] // 2
    capacity = slots // 2
    low = jnp.concatenate([lows[jnp.bitwise_xor(me, e)][:, 0:slots] for e in range(experts)], axis=0)
    own = own_expert(experts, capacity)
    expert = relative_experts(experts, tokens, me)
    earlier = (lax.broadcasted_iota(jnp.int32, (tokens, tokens), 0) < lax.broadcasted_iota(jnp.int32, (tokens, tokens), 1)).astype(BF)
    place = lax.broadcasted_iota(jnp.int32, (experts, capacity, tokens), 1).astype(F32)
    rows = []
    for s in range(2):
        meta = (own_meta if s == 0 else far_meta)[...].astype(F32)
        first = (meta[0:1] == expert).astype(F32)
        second = (meta[1:2] == expert).astype(F32)
        before = mm((first + second).astype(BF), earlier)
        gate = first * meta[2:3] + second * meta[3:4]
        spread = jnp.where(before[:, None, :] == place, gate[:, None, :], 0.0)
        weights = spread.reshape(experts * capacity, tokens).astype(BF)
        source = jnp.bitwise_xor(core, s)
        wide = mm(low, fold_of(slots, experts, capacity, source))
        wide = jnp.where(own, wide, 0.0).astype(BF)
        exact = mm(wide, weights)
        rows.append(exact.astype(BF))
        if s == 0:
            w_out[...] = weights
            ordered = jnp.concatenate([exact[e * RANK:(e + 1) * RANK] for e in order], axis=0)
            z_out[...] = ordered.T.astype(BF)
    return rows

def product_of(rows, tokens_in, here, keep, send):
    count = keep.shape[0]
    total = mm(rows, tokens_in[:, here])
    keep[...] = total[0:count]
    send[...] = total[count:].astype(send.dtype)

def token_copies(where, cot, packed, tokens_in, sems):
    half, tokens = tokens_in.shape[1], cot.shape[0]
    here = lanes(where[1] * half, half)
    copies = [
        pltpu.make_async_copy(cot.at[:, here], tokens_in.at[0:tokens, :], sems.at[0]),
        pltpu.make_async_copy(packed.at[:, here], tokens_in.at[tokens : 2 * tokens, :], sems.at[1]),
    ]
    for copy in copies:
        copy.start()
    return copies

def partial_kernel(order, where, cot, packed, own_meta, far_meta, lows, z_out, w_out, *outs):
    keeps, sends = outs[:CHUNKS], outs[CHUNKS : 2 * CHUNKS]
    tokens_in, sems = outs[2 * CHUNKS :]
    copies = token_copies(where, cot, packed, tokens_in, sems)
    rows = weights_of(where, order, own_meta, far_meta, lows, z_out, w_out)
    rows = jnp.concatenate(rows, axis=1)
    count, depth = keeps[0].shape[0], rows.shape[1]
    rows = rows.reshape(count // (2 * RANK), 2, 2 * RANK, depth)
    rows = jnp.concatenate([rows[:, side].reshape(count, depth) for side in range(2)], axis=0)
    for copy in copies:
        copy.wait()
    base = 0
    for keep, send in zip(keeps, sends):
        here = slice(base, base + keep.shape[1])
        base += keep.shape[1]
        product_of(rows, tokens_in, here, keep, send)

def fold_step_kernel(received, keep, *refs):
    sends, kept = (refs[received:-1], refs[-1])
    rows, width = keep.shape
    radix = 1 + len(sends)
    total = keep[...]
    for more in refs[:received]:
        total = total + more[...].astype(F32)
    total = total.reshape(rows // (2 * RANK * radix), radix, 2 * RANK, width)
    kept[...] = total[:, 0].reshape(kept.shape)
    for i, send in enumerate(sends):
        send[...] = total[:, i + 1].reshape(send.shape).astype(send.dtype)

def last_fold_kernel(keep, *refs):
    received, (kept, sent) = (refs[:-2], refs[-2:])
    total = keep[...]
    for more in received:
        total = total + more[...].astype(F32)
    kept[...] = total[0:RANK]
    sent[...] = total[RANK:]

def factor_half(flip, side, cot, z, factors, delta, scratch):
    tokens_in, table, result, sems = scratch
    pieces, tokens, cut = tokens_in.shape
    base = jnp.bitwise_xor(side, flip) * (pieces * cut)
    copies = []
    for piece in range(pieces):
        moves = [(cot.at[:, lanes(base + piece * cut, cut)], tokens_in.at[piece])]
        start = 0
        for factor in factors:
            size = factor.shape[0]
            source = factor.at[:, piece * cut:(piece + 1) * cut]
            moves.append((source, table.at[piece, start:start + size, :]))
            start += size
        copies.append([pltpu.make_async_copy(source, target, sems.at[piece, i]) for i, (source, target) in enumerate(moves)])
        for copy in copies[-1]:
            copy.start()
    coords = jnp.zeros((start, tokens), F32)
    writes = []
    for piece in range(pieces):
        for copy in copies[piece]:
            copy.wait()
        block = table[piece]
        result[piece] = mm(z[...], block).astype(BF)
        target = delta.at[:, lanes(base + piece * cut, cut)]
        writes.append(pltpu.make_async_copy(result.at[piece], target, sems.at[piece, len(factors) + 1]))
        writes[-1].start()
        coords = coords + mm(block, tokens_in[piece], 1, 1)
    return (coords, writes)

def near_kernel(where, cot, z, *refs):
    factors, (coords_out, delta), scratch = (refs[:-6], refs[-6:-4], refs[-4:])
    coords_out[...], copies = factor_half(0, where[2], cot, z, factors, delta, scratch)
    for copy in copies:
        copy.wait()

def far_kernel(order, where, cot, z, w, near, _, *refs):
    factors, (coords_out, delta), scratch = (refs[:-6], refs[-6:-4], refs[-4:])
    experts, _, slots = coords_out.shape
    capacity = slots // 4
    coords, copies = factor_half(1, where[2], cot, z, factors, delta, scratch)
    coords = coords + near[...]
    blocks = [order.index(e) * RANK for e in range(experts)]
    coords = jnp.concatenate([coords[b:b + RANK] for b in blocks], axis=0)
    high, low = split(coords)
    picked = mm(high, w[...], 1, 1) + mm(low, w[...], 1, 1)
    picked = jnp.where(own_expert(experts, capacity), picked, 0.0).astype(BF)
    fold = fold_of(slots, experts, capacity, lax.rem(where[0], 4))
    rows = mm(picked, fold, 1, 1).astype(coords_out.dtype)
    for e in range(experts):
        coords_out[jnp.bitwise_xor(where[0], e)] = rows[e * RANK:(e + 1) * RANK]
    for copy in copies:
        copy.wait()

def inverse_kernel(a_in, a_out, lows, inv_in, inv_out):
    experts, _, double = lows.shape
    stats = jnp.sum(lows[:, :, double // 2:].astype(F32), axis=0)
    row = lax.broadcasted_iota(jnp.int32, (RANK, RANK), 0)
    column = lax.broadcasted_iota(jnp.int32, (RANK, RANK), 1)
    eye = (row == column).astype(F32)
    works = []
    for base, factor in ((0, a_in), (3, a_out)):
        pieces = stats[base:base + 1, 0:1] + stats[base + 1:base + 2, 0:1]
        damp = (pieces + stats[base + 2:base + 3, 0:1]) / (float(RANK) * experts)
        gram = mm(factor[...], factor[...], 1, 1) + damp * eye
        works.append([gram, eye])
    for j in range(RANK):
        for work in works:
            gram, inverse = work
            pivot = 1.0 / gram[j:j + 1, j:j + 1]
            gram_row, inverse_row = (gram[j:j + 1] * pivot, inverse[j:j + 1] * pivot)
            scale = gram[:, j:j + 1]
            work[0] = jnp.where(row == j, gram_row, gram - scale * gram_row)
            work[1] = jnp.where(row == j, inverse_row, inverse - scale * inverse_row)
    inv_in[...] = works[0][1]
    inv_out[...] = works[1][1]

def scaled_in_kernel(coords, hidden, inverse, out):
    pieces = []
    for base in range(0, coords.shape[0], 4):
        total = coords[base].astype(F32)
        for q in range(1, 4):
            total = total + coords[base + q].astype(F32)
        pieces.append(total)
    grad_low = jnp.concatenate(pieces, axis=1).astype(BF)
    high, low = split(mm(inverse[...], grad_low.astype(F32), precision=HIGHEST))
    both = mm(jnp.concatenate([high, low], axis=0), hidden[...])
    out[...] = both[0:RANK] + both[RANK:]

def scaled_out_kernel(where, inverse, *refs):
    pieces, (out, rows, sems) = (refs[:-3], refs[-3:])
    half = out.shape[1] // 2
    copies, starts = ([], [0, 0])
    for i, piece in enumerate(pieces):
        flip, width = (i % 2, piece.shape[1])
        base = jnp.bitwise_xor(where[1], flip) * half + starts[flip]
        starts[flip] += width
        rows[i, :, 0:width] = mm(inverse[...], piece[...], precision=HIGHEST)
        target = out.at[:, lanes(base, width)]
        copies.append(pltpu.make_async_copy(rows.at[i, :, 0:width], target, sems.at[i]))
        copies[-1].start()
    for copy in copies:
        copy.wait()

def radix_groups(experts):
    groups, bit = ([], 4)
    while bit < experts:
        radix = min(4, experts // bit)
        groups.append([bit * k for k in range(1, radix)])
        bit *= radix
    return groups

def relative_order(bits):
    order = [0]
    for bit in bits:
        order = order + [e ^ bit for e in order]
    return order

def on_device(hidden_slots, adapter_in, adapter_out, expert_ids, gate_weights, cotangent):
    experts, groups = (lax.axis_size('expert'), lax.axis_size('group'))
    me, group = (lax.axis_index('expert'), lax.axis_index('group'))
    where = jnp.stack([me, me % 2, group % 2]).astype(jnp.int32)
    hidden, a_in, a_out = (hidden_slots[0], adapter_in[0], adapter_out[0])
    width = a_out.shape[1]
    half = width // 2
    tokens = cotangent.shape[0]
    capacity = hidden.shape[0] // experts
    struct = jax.ShapeDtypeStruct

    def swap(x, bit):
        return lax.ppermute(x, 'expert', [(i, i ^ bit) for i in range(experts)])

    def swap_side(x):
        return lax.ppermute(x, 'group', [(i, i ^ 1) for i in range(groups)])

    def spread(x):
        return lax.all_to_all(x, 'expert', split_axis=0, concat_axis=0, tiled=True)
    groups_z = radix_groups(experts)
    far_bits = [1 << i for i in reversed(range(2, experts.bit_length() - 1))]
    full = relative_order([2, *far_bits, 1])
    block = lax.dynamic_slice_in_dim(a_out, group % 2 * half, half, axis=1)
    received = swap(block, 2)
    low, = call(low_slots_kernel, [struct((experts, RANK, 4 * capacity), BF)], [hidden, a_in, a_out], scratch=[VMEM(hidden.shape, BF), VMEM(a_in.shape, BF), VMEM(a_out.shape, BF), DMA((2 + 2,))], spaces=[HBM] * 3, limit=63 * MIB)
    far_tokens = swap(cotangent, 1)
    own_meta = jnp.concatenate([expert_ids.T.astype(BF), gate_weights.T.astype(BF), jnp.zeros((12, tokens), BF)], axis=0)
    far_meta = swap(own_meta, 1)
    block, = call(join_kernel, [struct((2 * RANK, half), BF)], [block, received], after=[low])
    lows, = call(copy_kernel, [low], [low], after=[block])
    lows = spread(lows)
    inv_in, inv_out = call(inverse_kernel, [struct((RANK, RANK), F32)] * 2, [a_in, a_out, lows])
    count = experts * RANK // 2

    def planes_of(block, gate):
        pieces = block
        for bit in far_bits:
            if bit == far_bits[-1]:
                return ([block, swap(block, bit)], last)
            last = pieces + [swap(piece, bit) for piece in pieces]
            block, = call(join_kernel, [struct((2 * sum((piece.shape[0] for piece in pieces)), half), BF)], last, after=gate)
            pieces = [block]
    near, last = planes_of([block], [lows])
    tiles = half // 128
    wides = [128 * (tiles // 2), half - 128 * (tiles // 2)]
    token_args = [cotangent, far_tokens, own_meta, far_meta, lows]
    token_scratch = [VMEM((2 * tokens, half), BF), DMA((2,))]
    shapes = [struct((tokens, experts * RANK), BF), struct((experts * capacity, tokens), BF)]
    z, weights, *parts = call(lambda *refs: partial_kernel(full, *refs), shapes + [struct((count, wide), F32) for wide in wides] + [struct((count, wide), BF) for wide in wides], token_args, where, after=[near[0]], scratch=token_scratch, spaces=[HBM, pl.ANY, VMEM, VMEM, VMEM])
    kept, sent = (parts[:CHUNKS], parts[CHUNKS:])

    def fold_y(piece, gate):
        group = groups_z[0]
        wide = wides[piece]
        rows = count // (1 + len(group))
        return list(call(lambda keep, *refs: fold_step_kernel(1, keep, *refs), [struct((rows, wide), BF)] * len(group) + [struct((rows, wide), F32)], [kept[piece], swap(sent[piece], 2)], after=gate))
    far = [swap_side(near[0])]
    near[1:] = call(join_kernel, [struct(near[1].shape, BF)], [near[1]], after=[sent[0], inv_in, far[0]])
    factors = list(near)
    far.append(swap_side(near[1]))
    factors += [swap(block, 1) for block in near]
    far += [swap(block, 1) for block in far]
    cuts = 2
    scratch = [VMEM((cuts, tokens, half // cuts), BF), VMEM((cuts, experts * RANK, half // cuts), BF), VMEM((cuts, tokens, half // cuts), BF), DMA((cuts, 2 * len(far) + 2))]
    near_coords, delta = call(near_kernel, [struct((experts * RANK, tokens), F32), struct((tokens, width), BF)], [cotangent, z, *factors], where, scratch=scratch, spaces=[HBM, VMEM] + [HBM] * len(factors), out_spaces=[VMEM, HBM])
    own_rows, far_rows, ends = ([], [], [])
    folds = [None, fold_y(1, [near_coords, far[1]])]
    for piece in range(CHUNKS):
        rows, wide = (count, wides[piece])
        keep = kept[piece]
        for n, group in enumerate(groups_z):
            radix = 1 + len(group)
            rows //= radix
            if n == 0 and folds[piece]:
                *sends, keep = folds[piece]
            else:
                total = keep
                for more in received if n else [swap(sent[piece], 2)]:
                    total = total + more.astype(F32)
                total = total.reshape(rows // (2 * RANK), radix, 2 * RANK, wide)
                keep = total[:, 0].reshape(rows, wide)
                sends = [total[:, k].reshape(rows, wide).astype(BF) for k in range(1, radix)]
            received = [swap(send, k) for send, k in zip(sends, group)]
        ends.append((keep, received))
        if piece == 0:
            for more in received:
                keep = keep + more.astype(F32)
            own_rows.append(keep[:RANK])
            far_rows.append(swap(keep[RANK:], 1))
    coords, delta = call(lambda *refs: far_kernel(full, *refs), [struct((experts, RANK, 4 * capacity), BF), struct((tokens, width), BF)], [cotangent, z, weights, near_coords, delta, *far], where, scratch=scratch, spaces=[HBM, VMEM, VMEM, VMEM, HBM] + [HBM] * len(far), out_spaces=[VMEM, HBM], alias={5: 1})
    keep, received = ends[1]
    keep, send = call(last_fold_kernel, [struct((RANK, wides[1]), F32)] * 2, [keep, *received], after=[coords])
    own_rows.append(keep)
    far_rows.append(swap(send, 1))
    coords = spread(coords)
    pieces = [rows for pair in zip(own_rows, far_rows) for rows in pair]
    scaled_out, = call(scaled_out_kernel, [struct((RANK, width), F32)], [inv_in, *pieces], where, scratch=[VMEM((len(pieces), RANK, max(wides)), F32), DMA((len(pieces),))], out_spaces=[HBM])
    scaled_in, = call(scaled_in_kernel, [struct((RANK, hidden.shape[1]), F32)], [coords, hidden, inv_out])
    return (delta, scaled_in[None], scaled_out[None])

def solution(mesh):
    every = ('group', 'expert')
    return jax.shard_map(on_device, mesh=mesh, in_specs=(P(every, None, None), P('expert', None, None), P('expert', None, None), P(every, None), P(every, None), P(every, None)), out_specs=(P(every, None), P(every, None, None), P(every, None, None)), check_vma=False)
```
